32 devices in a mesh: grp: 2 (over y), ctx: 4 (over z), head: 4 (over x, core).
Axes of the slice: x: 2, y: 2, z: 4, core: 2. Of those that a mesh axis runs over, the one named last changes fastest.
Arguments:
- queries: bfloat16 [1024, 4096], P(('grp', 'ctx', 'head')), parts along dimension 0, may hold values from -80 to 80
- span_key_value: bfloat16 [1024, 1024], P(('grp', 'ctx', 'head')), parts along dimension 0, may hold values from -4 to 4
- cache: bfloat16 [4, 16384, 256], P('head', ('grp', 'ctx')), parts along dimension 1, may hold values from -4 to 4
- pattern: int32 [8, 2], P('grp'), parts along dimension 0, may hold values from 0 to 63, as said below
- counts: int32 [8], P('grp'), parts along dimension 0, may hold values from 1 to 2
Outputs:
- attended: bfloat16 [1024, 4096], P(('grp', 'ctx', 'head')), parts along dimension 0
The draws below stay inside these ranges and needn't reach their ends.
There are 2 independent parts, one for each index of `grp`. The reference program is written for one: setup_inputs(seed, part) draws one part's arguments, and reference() takes and returns one part's arrays. A program takes and returns all parts, laid end to end along the dimension named above; each array names one. Nothing has to cross between parts.
Inputs may be any that keep to these rules, and one draw needn't show every extreme that they name: Entries of pattern[b, i] for i < counts[b] are distinct and no two have the same value of pattern[b, i] // 16; unused entries are 0.
All inputs are finite; a program needn't handle non-finite values.
Results may differ from the reference program's by a relative error of at most 0.0045.
Values may be sent and summed in bfloat16 or wider, within the bound.
No kernel may reach another device: no remote copies, remote signals or barrier semaphores. Data moves between devices by JAX's collectives and lax.ppermute only.
A program may use at most 64 MiB of HBM per device.

```python
import math
import jax
import jax.numpy as jnp
from jax import lax

QUERY_HEADS = 32
KEY_VALUE_HEADS = 4
HEAD_SIZE = 128
BLOCK_TOKENS = 128
SHARD_KEY_BLOCKS = 16
NQB = 4
LISTED_BLOCKS = 2
SPAN_TOKENS = 512
CACHED_TOKENS = 8192
N_CTX = 4


def place_first(shard_lists, local_blocks, row_index, shard_value, local_value):
    rows = jnp.arange(NQB)[:, None]
    columns = jnp.arange(LISTED_BLOCKS)[None, :]
    first_shard = shard_lists[row_index, 0]
    in_row = rows == row_index
    swapped = jnp.where(in_row & (shard_lists == shard_value), first_shard, shard_lists)
    swapped = jnp.where(in_row & (columns == 0), shard_value, swapped)
    placed = jnp.where(in_row & (columns == 0), local_value, local_blocks)
    return (swapped, placed)


def pattern_parts(key):
    base = jax.random.fold_in(key, 7)
    key_perm, key_local, key_count, key_full = jax.random.split(base, 4)
    shard_lists = jax.vmap(lambda k: jax.random.permutation(k, N_CTX))(jax.random.split(key_perm, NQB))[:, :LISTED_BLOCKS]
    local_blocks = jax.random.randint(key_local, (NQB, LISTED_BLOCKS), 0, SHARD_KEY_BLOCKS)
    row_counts = jax.random.randint(key_count, (NQB,), (LISTED_BLOCKS + 1) // 2, LISTED_BLOCKS + 1)
    full_row = jax.random.randint(key_full, (), 0, NQB)
    low_row = (full_row + 1) % NQB
    shard_lists, local_blocks = place_first(shard_lists, local_blocks, full_row, N_CTX - 1, SHARD_KEY_BLOCKS - 1)
    shard_lists, local_blocks = place_first(shard_lists, local_blocks, low_row, 0, 0)
    row_counts = jnp.where(jnp.arange(NQB) == full_row, LISTED_BLOCKS, row_counts)
    entry_list = shard_lists * SHARD_KEY_BLOCKS + local_blocks
    entry_list = jnp.where(jnp.arange(LISTED_BLOCKS)[None, :] < row_counts[:, None], entry_list, 0)
    return (entry_list.astype(jnp.int32), row_counts.astype(jnp.int32))


def draw_pattern(key, part):
    return pattern_parts(key)[0]


def draw_counts(key, part):
    return pattern_parts(key)[1]


def span_parts(key):
    base = jax.random.fold_in(key, 11)
    key_query, key_value_keys = jax.random.split(base, 2)
    query_values = 2.0 * jnp.clip(jax.random.normal(key_query, (SPAN_TOKENS, QUERY_HEADS, HEAD_SIZE), jnp.float32), -4.0, 4.0)
    key_value_rows = jnp.clip(jax.random.normal(key_value_keys, (SPAN_TOKENS, KEY_VALUE_HEADS, 2, HEAD_SIZE), jnp.float32), -4.0, 4.0)
    return (query_values.reshape(SPAN_TOKENS, QUERY_HEADS * HEAD_SIZE), key_value_rows.reshape(SPAN_TOKENS, KEY_VALUE_HEADS * 2 * HEAD_SIZE))


def draw_queries(key, part):
    return span_parts(key)[0].astype(jnp.bfloat16)


def draw_span_key_value(key, part):
    return span_parts(key)[1].astype(jnp.bfloat16)


def block_levels(rng, shape, pieces, smallest, high):
    loudness = 1.0
    for axis_at, shards_of in pieces:
        steps = jax.random.uniform(jax.random.fold_in(jax.random.fold_in(rng, 6), axis_at), (shards_of,), jnp.float32, smallest / len(pieces), high / len(pieces))
        loudness = loudness * jnp.repeat(jnp.exp(steps), shape[axis_at] // shards_of).reshape((-1,) + (1,) * (len(shape) - 1 - axis_at))
    return loudness


def scatter_about(stream_key, extent, deviation, most, shards=(), kind=jnp.bfloat16):
    values = jax.random.normal(stream_key, extent, jnp.float32) * deviation
    if len(shards) > 0:
        values = block_levels(stream_key, extent, shards, -0.22, 0.18) * values
    return jnp.clip(values, min=-most, max=most).astype(kind)


def setup_inputs(seed: int = 0, part: int = 0) -> dict:
    key_of = jax.random.split(jax.random.key(seed), 6)
    part_splits = jax.random.split(jax.random.fold_in(key_of[5], part), 6)
    queries = draw_queries(jax.random.fold_in(jax.random.fold_in(key_of[5], part), 71), part)
    span_key_value = draw_span_key_value(jax.random.fold_in(jax.random.fold_in(key_of[5], part), 71), part)
    cache = scatter_about(part_splits[2], (KEY_VALUE_HEADS, CACHED_TOKENS, 2 * HEAD_SIZE), 0.7, 4.0, ((0, 4), (1, 4)))
    pattern = draw_pattern(jax.random.fold_in(jax.random.fold_in(key_of[5], part), 71), part)
    counts = draw_counts(jax.random.fold_in(jax.random.fold_in(key_of[5], part), 71), part)
    return {"queries": queries, "span_key_value": span_key_value, "cache": cache, "pattern": pattern, "counts": counts}


def reference(queries, span_key_value, cache, pattern, counts):
    heads_per_group = QUERY_HEADS // KEY_VALUE_HEADS
    score_scale = 1.0 / math.sqrt(HEAD_SIZE)
    cache_block_list = cache.reshape(KEY_VALUE_HEADS, SHARD_KEY_BLOCKS * N_CTX, BLOCK_TOKENS, 2 * HEAD_SIZE)
    causal = jnp.arange(BLOCK_TOKENS)[:, None] >= jnp.arange(BLOCK_TOKENS)[None, :]

    def one_block(block_index):
        start_offset = (block_index * BLOCK_TOKENS).astype(jnp.int32)
        query_head_rows = lax.dynamic_slice_in_dim(queries, start_offset, BLOCK_TOKENS, 0).reshape(BLOCK_TOKENS, KEY_VALUE_HEADS, heads_per_group, HEAD_SIZE).astype(jnp.float32)
        self_key_value = lax.dynamic_slice_in_dim(span_key_value, start_offset, BLOCK_TOKENS, 0).reshape(BLOCK_TOKENS, KEY_VALUE_HEADS, 2 * HEAD_SIZE).transpose(1, 0, 2)
        entry_list = pattern[block_index]
        used = jnp.arange(LISTED_BLOCKS) < counts[block_index]
        picked_blocks = jnp.take(cache_block_list, entry_list, axis=1).reshape(KEY_VALUE_HEADS, LISTED_BLOCKS * BLOCK_TOKENS, 2 * HEAD_SIZE)
        all_kv = jnp.concatenate([picked_blocks, self_key_value], axis=1).astype(jnp.float32)
        slot_used = jnp.broadcast_to(jnp.repeat(used, BLOCK_TOKENS)[None, :], (BLOCK_TOKENS, LISTED_BLOCKS * BLOCK_TOKENS))
        allowed = jnp.concatenate([slot_used, causal], axis=1)
        scores = jnp.einsum('tgjd,gkd->gjtk', query_head_rows, all_kv[..., :HEAD_SIZE]) * score_scale
        masked = jnp.where(allowed, scores, -jnp.inf)
        top = lax.optimization_barrier(jnp.max(masked, axis=-1, keepdims=True))
        weights = jnp.where(allowed, jnp.exp(scores - top), 0.0)
        denom = lax.optimization_barrier(jnp.sum(weights, axis=-1))
        rounded = lax.optimization_barrier(weights.astype(jnp.bfloat16))
        summed = jnp.einsum('gjtk,gkd->gjtd', rounded.astype(jnp.float32), all_kv[..., HEAD_SIZE:])
        result = summed / denom[..., None]
        return result.transpose(2, 0, 1, 3).reshape(BLOCK_TOKENS, QUERY_HEADS * HEAD_SIZE).astype(jnp.bfloat16)
    outputs = lax.map(one_block, jnp.arange(NQB, dtype=jnp.int32))
    return outputs.reshape(SPAN_TOKENS, QUERY_HEADS * HEAD_SIZE)
```

```python
import functools
import math

import jax
import jax.numpy as jnp
from jax import lax
from jax.experimental import pallas as pl
from jax.experimental.pallas import tpu as pltpu
from jax.sharding import PartitionSpec as P

LOG2E = 1.4426950408889634
MAX_DIRECT = 4
ANY = pl.BlockSpec(memory_space=pl.ANY)
SMEM = pl.BlockSpec(memory_space=pltpu.SMEM)
VMEM = pl.BlockSpec(memory_space=pltpu.VMEM)


def wanted_index(pattern_ref, counts_ref, row, owner, shard_blocks):
    def one(i, found):
        entry = pattern_ref[row, i]
        match = (i < counts_ref[row]) & (entry // shard_blocks == owner)
        return jnp.where(match, entry % shard_blocks, found)

    width = pattern_ref.shape[1]
    if width <= 4:
        found = jnp.int32(0)
        for i in range(width):
            found = one(i, found)
        return found
    return lax.fori_loop(0, width, one, jnp.int32(0))


def pick_kernel(n_ctx, block, pattern_ref, counts_ref, cache_ref, *refs):
    outs, sem = refs[:n_ctx], refs[n_ctx]
    me = lax.axis_index("ctx")
    shard_blocks = cache_ref.shape[1] // block
    copies = []
    for k in list(range(1, n_ctx)) + [0]:
        row = lax.rem(me + k, n_ctx)
        index = wanted_index(pattern_ref, counts_ref, row, me, shard_blocks)
        start = pl.multiple_of(index * block, block)
        copy = pltpu.make_async_copy(cache_ref.at[0, pl.ds(start, block), :], outs[k], sem.at[k])
        copy.start()
        copies.append(copy)
    for copy in copies:
        copy.wait()


def split_kernel(n_head, q_ref, kv_ref, *refs):
    outs, sem = refs[:n_head], refs[n_head]
    h = lax.axis_index("head")
    q_cols, kv_cols = q_ref.shape[1] // n_head, kv_ref.shape[1] // n_head
    copies = []
    for m in range(n_head):
        peer = lax.bitwise_xor(h, m)
        for ref, cols, at, s in ((q_ref, q_cols, 0, 0), (kv_ref, kv_cols, q_cols, 1)):
            copy = pltpu.make_async_copy(
                ref.at[:, pl.ds(pl.multiple_of(peer * cols, cols), cols)],
                outs[m].at[:, pl.ds(at, cols)],
                sem.at[m, s],
            )
            copy.start()
            copies.append(copy)
    for copy in copies:
        copy.wait()


def attend_kernel(n_ctx, n_head, d, shard_blocks, pattern_ref, counts_ref, *refs):
    blocks, pieces, outs = refs[:n_ctx], refs[n_ctx : n_ctx + n_head], refs[n_ctx + n_head :]
    me, h = lax.axis_index("ctx"), lax.axis_index("head")
    rows = pieces[0].shape[0]
    q_cols = pieces[0].shape[1] - 2 * d
    group = q_cols // d
    width = pattern_ref.shape[1]
    block = blocks[0].shape[0]
    keys, values, slot_bias = [], [], []
    for i in range(width):
        offset = lax.rem(me - pattern_ref[me, i] // shard_blocks + n_ctx, n_ctx)
        kv = blocks[0][...]
        for k in range(1, n_ctx):
            kv = jnp.where(offset == k, blocks[k][...], kv)
        keys.append(kv[:, :d])
        values.append(kv[:, d:])
        slot_bias.append(jnp.where(i < counts_ref[me], 0.0, -jnp.inf).astype(jnp.float32))
    for m in range(n_head):
        keys.append(pieces[m][:, q_cols : q_cols + d])
        values.append(pieces[m][:, q_cols + d :])
    keys, values = jnp.concatenate(keys, axis=0), jnp.concatenate(values, axis=0)
    span = n_head * rows
    column = lax.broadcasted_iota(jnp.int32, (rows, span), 1)
    row = lax.broadcasted_iota(jnp.int32, (rows, span), 0)
    key_token = lax.bitwise_xor(column // rows, h) * rows + column % rows
    rate = LOG2E / math.sqrt(d)
    for m in range(n_head):
        q = jnp.concatenate([pieces[m][:, j * d : (j + 1) * d] for j in range(group)], axis=0)
        s = lax.dot_general(q, keys, (((1,), (1,)), ((), ())), preferred_element_type=jnp.float32)
        causal = jnp.where(lax.bitwise_xor(h, m) * rows + row >= key_token, 0.0, -jnp.inf)
        own = s[:, width * block :].reshape(group, rows, span) + causal[None]
        parts = [s[:, i * block : (i + 1) * block] + slot_bias[i] for i in range(width)]
        s = jnp.concatenate(parts + [own.reshape(group * rows, span)], axis=1)
        top = jnp.max(s, axis=1, keepdims=True)
        p = jnp.exp2((s - top) * rate)
        denom = jnp.sum(p, axis=1, keepdims=True)
        o = lax.dot_general(
            p.astype(jnp.bfloat16), values, (((1,), (0,)), ((), ())), preferred_element_type=jnp.float32
        )
        o = (o / denom).astype(jnp.bfloat16)
        for j in range(group):
            outs[m][:, j * d : (j + 1) * d] = o[j * rows : (j + 1) * rows]


def join_kernel(n_head, *refs):
    pieces, out, sem = refs[:n_head], refs[n_head], refs[n_head + 1]
    h = lax.axis_index("head")
    cols = pieces[0].shape[1]
    copies = []
    for m in range(n_head):
        start = pl.multiple_of(lax.bitwise_xor(h, m) * cols, cols)
        copy = pltpu.make_async_copy(pieces[m], out.at[:, pl.ds(start, cols)], sem.at[m])
        copy.start()
        copies.append(copy)
    for copy in copies:
        copy.wait()


def direct(n_ctx, n_head, queries, span_key_value, cache, pattern, counts):
    rows, d = queries.shape[0], cache.shape[2] // 2
    block = rows * n_head
    shard_blocks = cache.shape[1] // block
    q_cols, kv_cols = queries.shape[1] // n_head, span_key_value.shape[1] // n_head
    bf16 = jnp.bfloat16
    around = [[(i, (i + k) % n_ctx) for i in range(n_ctx)] for k in range(n_ctx)]
    across = [[(i, i ^ m) for i in range(n_head)] for m in range(n_head)]

    blocks = pl.pallas_call(
        functools.partial(pick_kernel, n_ctx, block),
        out_shape=[jax.ShapeDtypeStruct((block, 2 * d), bf16)] * n_ctx,
        in_specs=[SMEM, SMEM, ANY],
        out_specs=[ANY] * n_ctx,
        scratch_shapes=[pltpu.SemaphoreType.DMA((n_ctx,))],
        name="pick",
    )(pattern, counts, cache)
    pieces = pl.pallas_call(
        functools.partial(split_kernel, n_head),
        out_shape=[jax.ShapeDtypeStruct((rows, q_cols + kv_cols), bf16)] * n_head,
        in_specs=[ANY, ANY],
        out_specs=[ANY] * n_head,
        scratch_shapes=[pltpu.SemaphoreType.DMA((n_head, 2))],
        name="split",
    )(queries, span_key_value)
    blocks, pieces = list(blocks), list(pieces)
    for k in range(1, n_ctx):
        blocks[k] = lax.ppermute(blocks[k], "ctx", around[k])
    for m in (2, 3, 1):
        pieces[m] = lax.ppermute(pieces[m], "head", across[m])
    outs = pl.pallas_call(
        functools.partial(attend_kernel, n_ctx, n_head, d, shard_blocks),
        out_shape=[jax.ShapeDtypeStruct((rows, q_cols), bf16)] * n_head,
        in_specs=[SMEM, SMEM] + [VMEM] * (n_ctx + n_head),
        out_specs=[VMEM] * n_head,
        name="attend",
    )(pattern, counts, *blocks, *pieces)
    outs = list(outs)
    for m in (2, 3, 1):
        outs[m] = lax.ppermute(outs[m], "head", across[m])
    return pl.pallas_call(
        functools.partial(join_kernel, n_head),
        out_shape=jax.ShapeDtypeStruct((rows, q_cols * n_head), bf16),
        in_specs=[ANY] * n_head,
        out_specs=ANY,
        scratch_shapes=[pltpu.SemaphoreType.DMA((n_head,))],
        name="join",
    )(*outs)


def collect_kernel(n_ctx, block, pattern_ref, counts_ref, cache_ref, out_ref, sem):
    me = lax.axis_index("ctx")
    shard_blocks = cache_ref.shape[1] // block

    @pl.loop(0, n_ctx)
    def _(row):
        index = wanted_index(pattern_ref, counts_ref, row, me, shard_blocks)
        start = pl.multiple_of(index * block, block)
        copy = pltpu.make_async_copy(cache_ref.at[0, pl.ds(start, block), :], out_ref.at[row], sem)
        copy.start()
        copy.wait()


def slots_kernel(shard_blocks, pattern_ref, in_ref, out_ref, sem):
    me = lax.axis_index("ctx")

    @pl.loop(0, pattern_ref.shape[1])
    def _(i):
        copy = pltpu.make_async_copy(in_ref.at[pattern_ref[me, i] // shard_blocks], out_ref.at[i], sem)
        copy.start()
        copy.wait()


def absorb(carried, q, kv, allowed, scale):
    running_max, denom, weighted = carried
    d = q.shape[-1]
    scores = jnp.einsum("tjd,kd->jtk", q, kv[:, :d], preferred_element_type=jnp.float32) * scale
    masked = jnp.where(allowed, scores, -jnp.inf)
    new_max = jnp.maximum(running_max, jnp.max(masked, axis=-1))
    factor = jnp.exp(running_max - new_max)
    weights = jnp.where(allowed, jnp.exp(scores - new_max[..., None]), 0.0)
    denom = denom * factor + jnp.sum(weights, axis=-1)
    weighted = weighted * factor[..., None] + jnp.einsum(
        "jtk,kd->jtd", weights.astype(jnp.bfloat16), kv[:, d:], preferred_element_type=jnp.float32
    )
    return new_max, denom, weighted


def general(n_ctx, n_head, queries, span_key_value, cache, pattern, counts):
    d = cache.shape[2] // 2
    block = queries.shape[0] * n_head
    shard_blocks = cache.shape[1] // block
    width = pattern.shape[1]
    q = lax.all_to_all(queries, "head", split_axis=1, concat_axis=0, tiled=True)
    kv = lax.all_to_all(span_key_value, "head", split_axis=1, concat_axis=0, tiled=True)
    outgoing = pl.pallas_call(
        functools.partial(collect_kernel, n_ctx, block),
        out_shape=jax.ShapeDtypeStruct((n_ctx, block, 2 * d), jnp.bfloat16),
        in_specs=[SMEM, SMEM, ANY],
        out_specs=ANY,
        scratch_shapes=[pltpu.SemaphoreType.DMA],
        name="collect",
    )(pattern, counts, cache)
    incoming = lax.all_to_all(outgoing, "ctx", split_axis=0, concat_axis=0, tiled=True)
    slots = pl.pallas_call(
        functools.partial(slots_kernel, shard_blocks),
        out_shape=jax.ShapeDtypeStruct((width, block, 2 * d), jnp.bfloat16),
        in_specs=[SMEM, ANY],
        out_specs=ANY,
        scratch_shapes=[pltpu.SemaphoreType.DMA],
        name="slots",
    )(pattern, incoming)
    count = lax.dynamic_index_in_dim(counts, lax.axis_index("ctx"), 0, keepdims=False)
    group = q.shape[1] // d
    q = q.reshape(block, group, d)
    scale = 1.0 / math.sqrt(d)
    carried = (
        jnp.full((group, block), -jnp.inf, jnp.float32),
        jnp.zeros((group, block), jnp.float32),
        jnp.zeros((group, block, d), jnp.float32),
    )
    causal = jnp.arange(block)[:, None] >= jnp.arange(block)[None, :]
    carried = absorb(carried, q, kv, causal, scale)
    batch = math.gcd(width, 4)

    def step(at, carried):
        some = lax.dynamic_slice_in_dim(slots, at * batch, batch, 0).reshape(batch * block, 2 * d)
        usable = at * batch + jnp.arange(batch * block) // block < count
        return absorb(carried, q, some, usable, scale)

    _, denom, weighted = lax.fori_loop(0, width // batch, step, carried)
    result = (weighted / denom[..., None]).transpose(1, 0, 2).reshape(block, group * d)
    return lax.all_to_all(result.astype(jnp.bfloat16), "head", split_axis=0, concat_axis=1, tiled=True)


def solution(mesh):
    n_ctx, n_head = mesh.shape["ctx"], mesh.shape["head"]
    form = direct if n_ctx <= MAX_DIRECT else general
    return jax.shard_map(
        functools.partial(form, n_ctx, n_head),
        mesh=mesh,
        in_specs=(
            P(("grp", "ctx", "head"), None),
            P(("grp", "ctx", "head"), None),
            P("head", ("grp", "ctx"), None),
            P("grp", None),
            P("grp"),
        ),
        out_specs=P(("grp", "ctx", "head"), None),
        check_vma=False,
    )
```

```python
import functools
import math

import jax
import jax.numpy as jnp
from jax import lax
from jax.experimental import pallas as pl
from jax.experimental.pallas import tpu as pltpu
from jax.sharding import PartitionSpec as P

LOG2E = 1.4426950408889634
MAX_DIRECT = 4
ANY = pl.BlockSpec(memory_space=pl.ANY)
SMEM = pl.BlockSpec(memory_space=pltpu.SMEM)
VMEM = pl.BlockSpec(memory_space=pltpu.VMEM)


def vmem(x):
    return pltpu.with_memory_space_constraint(x, pltpu.VMEM)


def wanted_index(pattern_ref, counts_ref, row, owner, shard_blocks):
    def one(i, found):
        entry = pattern_ref[i, row]
        match = (i < counts_ref[row]) & (entry // shard_blocks == owner)
        return jnp.where(match, entry % shard_blocks, found)

    width = pattern_ref.shape[0]
    if width <= 4:
        found = jnp.int32(0)
        for i in range(width):
            found = one(i, found)
        return found
    return lax.fori_loop(0, width, one, jnp.int32(0))


def pick_kernel(n_ctx, block, pattern_ref, counts_ref, cache_ref, *refs):
    outs, sem = refs[:n_ctx], refs[n_ctx]
    me = lax.axis_index("ctx")
    shard_blocks = cache_ref.shape[1] // block
    copies = []
    for k in list(range(1, n_ctx)) + [0]:
        row = lax.rem(me + k, n_ctx)
        index = wanted_index(pattern_ref, counts_ref, row, me, shard_blocks)
        start = pl.multiple_of(index * block, block)
        copy = pltpu.make_async_copy(cache_ref.at[0, pl.ds(start, block), :], outs[k], sem.at[k])
        copy.start()
        copies.append(copy)
    for copy in copies:
        copy.wait()


def split_kernel(n_head, q_ref, kv_ref, *refs):
    outs, sem = refs[:n_head], refs[n_head]
    h = lax.axis_index("head")
    q_cols, kv_cols = q_ref.shape[1] // n_head, kv_ref.shape[1] // n_head
    copies = []
    for m in range(n_head):
        peer = lax.bitwise_xor(h, m)
        for ref, cols, at, s in ((q_ref, q_cols, 0, 0), (kv_ref, kv_cols, q_cols, 1)):
            copy = pltpu.make_async_copy(
                ref.at[:, pl.ds(pl.multiple_of(peer * cols, cols), cols)],
                outs[m].at[:, pl.ds(at, cols)],
                sem.at[m, s],
            )
            copy.start()
            copies.append(copy)
    for copy in copies:
        copy.wait()


def attend_kernel(n_ctx, n_head, d, shard_blocks, pattern_ref, counts_ref, *refs):
    blocks, pieces, outs = refs[:n_ctx], refs[n_ctx : n_ctx + n_head], refs[n_ctx + n_head :]
    me, h = lax.axis_index("ctx"), lax.axis_index("head")
    rows = pieces[0].shape[0]
    q_cols = pieces[0].shape[1] - 2 * d
    group = q_cols // d
    width = pattern_ref.shape[0]
    block = blocks[0].shape[0]
    keys, values, slot_bias = [], [], []
    for i in range(width):
        offset = lax.rem(me - pattern_ref[i, me] // shard_blocks + n_ctx, n_ctx)
        kv = blocks[0][...]
        for k in range(1, n_ctx):
            kv = jnp.where(offset == k, blocks[k][...], kv)
        keys.append(kv[:, :d])
        values.append(kv[:, d:])
        slot_bias.append(jnp.where(i < counts_ref[me], 0.0, -jnp.inf).astype(jnp.float32))
    for m in range(n_head):
        keys.append(pieces[m][:, q_cols : q_cols + d])
        values.append(pieces[m][:, q_cols + d :])
    keys, values = jnp.concatenate(keys, axis=0), jnp.concatenate(values, axis=0)
    span = n_head * rows
    column = lax.broadcasted_iota(jnp.int32, (rows, span), 1)
    row = lax.broadcasted_iota(jnp.int32, (rows, span), 0)
    key_token = lax.bitwise_xor(column // rows, h) * rows + column % rows
    rate = LOG2E / math.sqrt(d)
    for m in range(n_head):
        q = jnp.concatenate([pieces[m][:, j * d : (j + 1) * d] for j in range(group)], axis=0)
        s = lax.dot_general(q, keys, (((1,), (1,)), ((), ())), preferred_element_type=jnp.float32)
        causal = jnp.where(lax.bitwise_xor(h, m) * rows + row >= key_token, 0.0, -jnp.inf)
        own = s[:, width * block :].reshape(group, rows, span) + causal[None]
        parts = [s[:, i * block : (i + 1) * block] + slot_bias[i] for i in range(width)]
        s = jnp.concatenate(parts + [own.reshape(group * rows, span)], axis=1)
        top = jnp.max(s, axis=1, keepdims=True)
        p = jnp.exp2((s - top) * rate)
        denom = jnp.sum(p, axis=1, keepdims=True)
        o = lax.dot_general(
            p.astype(jnp.bfloat16), values, (((1,), (0,)), ((), ())), preferred_element_type=jnp.float32
        )
        o = (o / denom).astype(jnp.bfloat16)
        for j in range(group):
            outs[m][:, j * d : (j + 1) * d] = o[j * rows : (j + 1) * rows]


def join_kernel(n_head, *refs):
    pieces, out, sem = refs[:n_head], refs[n_head], refs[n_head + 1]
    h = lax.axis_index("head")
    cols = pieces[0].shape[1]
    copies = []
    for m in range(n_head):
        start = pl.multiple_of(lax.bitwise_xor(h, m) * cols, cols)
        copy = pltpu.make_async_copy(pieces[m], out.at[:, pl.ds(start, cols)], sem.at[m])
        copy.start()
        copies.append(copy)
    for copy in copies:
        copy.wait()


def direct(n_ctx, n_head, queries, span_key_value, cache, pattern, counts):
    rows, d = queries.shape[0], cache.shape[2] // 2
    block = rows * n_head
    shard_blocks = cache.shape[1] // block
    q_cols, kv_cols = queries.shape[1] // n_head, span_key_value.shape[1] // n_head
    bf16 = jnp.bfloat16
    around = [[(i, (i + k) % n_ctx) for i in range(n_ctx)] for k in range(n_ctx)]
    across = [[(i, i ^ m) for i in range(n_head)] for m in range(n_head)]

    blocks = pl.pallas_call(
        functools.partial(pick_kernel, n_ctx, block),
        out_shape=[pltpu.VMEM((block, 2 * d), bf16)] * n_ctx,
        in_specs=[SMEM, SMEM, ANY],
        out_specs=[VMEM] * n_ctx,
        scratch_shapes=[pltpu.SemaphoreType.DMA((n_ctx,))],
        name="pick",
    )(pattern.T, counts, cache)
    pieces = pl.pallas_call(
        functools.partial(split_kernel, n_head),
        out_shape=[pltpu.VMEM((rows, q_cols + kv_cols), bf16)] * n_head,
        in_specs=[ANY, ANY],
        out_specs=[VMEM] * n_head,
        scratch_shapes=[pltpu.SemaphoreType.DMA((n_head, 2))],
        name="split",
    )(queries, span_key_value)
    blocks, pieces = list(blocks), list(pieces)
    for k in range(1, n_ctx):
        blocks[k] = lax.ppermute(blocks[k], "ctx", around[k])
    for m in (2, 3, 1):
        pieces[m] = lax.ppermute(pieces[m], "head", across[m])
    outs = pl.pallas_call(
        functools.partial(attend_kernel, n_ctx, n_head, d, shard_blocks),
        out_shape=[pltpu.VMEM((rows, q_cols), bf16)] * n_head,
        in_specs=[SMEM, SMEM] + [VMEM] * (n_ctx + n_head),
        out_specs=[VMEM] * n_head,
        name="attend",
    )(pattern.T, counts, *map(vmem, blocks + pieces))
    outs = list(outs)
    for m in (2, 3, 1):
        outs[m] = lax.ppermute(outs[m], "head", across[m])
    return pl.pallas_call(
        functools.partial(join_kernel, n_head),
        out_shape=jax.ShapeDtypeStruct((rows, q_cols * n_head), bf16),
        in_specs=[VMEM] * n_head,
        out_specs=ANY,
        scratch_shapes=[pltpu.SemaphoreType.DMA((n_head,))],
        name="join",
    )(*map(vmem, outs))


def collect_kernel(n_ctx, block, pattern_ref, counts_ref, cache_ref, out_ref, sem):
    me = lax.axis_index("ctx")
    shard_blocks = cache_ref.shape[1] // block

    @pl.loop(0, n_ctx)
    def _(row):
        index = wanted_index(pattern_ref, counts_ref, row, me, shard_blocks)
        start = pl.multiple_of(index * block, block)
        copy = pltpu.make_async_copy(cache_ref.at[0, pl.ds(start, block), :], out_ref.at[row], sem)
        copy.start()
        copy.wait()


def slots_kernel(shard_blocks, pattern_ref, in_ref, out_ref, sem):
    me = lax.axis_index("ctx")

    @pl.loop(0, pattern_ref.shape[0])
    def _(i):
        copy = pltpu.make_async_copy(in_ref.at[pattern_ref[i, me] // shard_blocks], out_ref.at[i], sem)
        copy.start()
        copy.wait()


def absorb(carried, q, kv, allowed, scale):
    running_max, denom, weighted = carried
    d = q.shape[-1]
    scores = jnp.einsum("tjd,kd->jtk", q, kv[:, :d], preferred_element_type=jnp.float32) * scale
    masked = jnp.where(allowed, scores, -jnp.inf)
    new_max = jnp.maximum(running_max, jnp.max(masked, axis=-1))
    factor = jnp.exp(running_max - new_max)
    weights = jnp.where(allowed, jnp.exp(scores - new_max[..., None]), 0.0)
    denom = denom * factor + jnp.sum(weights, axis=-1)
    weighted = weighted * factor[..., None] + jnp.einsum(
        "jtk,kd->jtd", weights.astype(jnp.bfloat16), kv[:, d:], preferred_element_type=jnp.float32
    )
    return new_max, denom, weighted


def general(n_ctx, n_head, queries, span_key_value, cache, pattern, counts):
    d = cache.shape[2] // 2
    block = queries.shape[0] * n_head
    shard_blocks = cache.shape[1] // block
    width = pattern.shape[1]
    q = lax.all_to_all(queries, "head", split_axis=1, concat_axis=0, tiled=True)
    kv = lax.all_to_all(span_key_value, "head", split_axis=1, concat_axis=0, tiled=True)
    outgoing = pl.pallas_call(
        functools.partial(collect_kernel, n_ctx, block),
        out_shape=jax.ShapeDtypeStruct((n_ctx, block, 2 * d), jnp.bfloat16),
        in_specs=[SMEM, SMEM, ANY],
        out_specs=ANY,
        scratch_shapes=[pltpu.SemaphoreType.DMA],
        name="collect",
    )(pattern.T, counts, cache)
    incoming = lax.all_to_all(outgoing, "ctx", split_axis=0, concat_axis=0, tiled=True)
    slots = pl.pallas_call(
        functools.partial(slots_kernel, shard_blocks),
        out_shape=jax.ShapeDtypeStruct((width, block, 2 * d), jnp.bfloat16),
        in_specs=[SMEM, ANY],
        out_specs=ANY,
        scratch_shapes=[pltpu.SemaphoreType.DMA],
        name="slots",
    )(pattern.T, incoming)
    count = lax.dynamic_index_in_dim(counts, lax.axis_index("ctx"), 0, keepdims=False)
    group = q.shape[1] // d
    q = q.reshape(block, group, d)
    scale = 1.0 / math.sqrt(d)
    carried = (
        jnp.full((group, block), -jnp.inf, jnp.float32),
        jnp.zeros((group, block), jnp.float32),
        jnp.zeros((group, block, d), jnp.float32),
    )
    causal = jnp.arange(block)[:, None] >= jnp.arange(block)[None, :]
    carried = absorb(carried, q, kv, causal, scale)
    batch = math.gcd(width, 4)

    def step(at, carried):
        some = lax.dynamic_slice_in_dim(slots, at * batch, batch, 0).reshape(batch * block, 2 * d)
        usable = at * batch + jnp.arange(batch * block) // block < count
        return absorb(carried, q, some, usable, scale)

    _, denom, weighted = lax.fori_loop(0, width // batch, step, carried)
    result = (weighted / denom[..., None]).transpose(1, 0, 2).reshape(block, group * d)
    return lax.all_to_all(result.astype(jnp.bfloat16), "head", split_axis=0, concat_axis=1, tiled=True)


def solution(mesh):
    n_ctx, n_head = mesh.shape["ctx"], mesh.shape["head"]
    form = direct if n_ctx <= MAX_DIRECT else general
    return jax.shard_map(
        functools.partial(form, n_ctx, n_head),
        mesh=mesh,
        in_specs=(
            P(("grp", "ctx", "head"), None),
            P(("grp", "ctx", "head"), None),
            P("head", ("grp", "ctx"), None),
            P("grp", None),
            P("grp"),
        ),
        out_specs=P(("grp", "ctx", "head"), None),
        check_vma=False,
    )
```

```python
import functools
import math

import jax
import jax.numpy as jnp
from jax import lax
from jax.experimental import pallas as pl
from jax.experimental.pallas import tpu as pltpu
from jax.sharding import PartitionSpec as P

LOG2E = 1.4426950408889634
MAX_DIRECT = 4
UNUSED = 1 << 20
FEED = (("ctx", 1), ("ctx", 2), ("ctx", 3), ("head", 2), ("head", 3), ("head", 1))
STAGES = ((2, 3, 1, 0),)
ANY = pl.BlockSpec(memory_space=pl.ANY)
SMEM = pl.BlockSpec(memory_space=pltpu.SMEM)
VMEM = pl.BlockSpec(memory_space=pltpu.VMEM)


def vmem(x):
    return pltpu.with_memory_space_constraint(x, pltpu.VMEM)


def wanted_index(pattern_ref, counts_ref, row, owner, shard_blocks):
    def one(i, found):
        entry = pattern_ref[i, row]
        match = (i < counts_ref[row]) & (entry // shard_blocks == owner)
        return jnp.where(match, entry % shard_blocks, found)

    width = pattern_ref.shape[0]
    if width <= 4:
        found = jnp.int32(0)
        for i in range(width):
            found = one(i, found)
        return found
    return lax.fori_loop(0, width, one, jnp.int32(0))


def prepare_kernel(n_ctx, n_head, pattern_hbm, counts_hbm, cache_ref, q_ref, kv_ref, *refs):
    blocks, pieces = refs[:n_ctx], refs[n_ctx : n_ctx + n_head]
    slots_ref, pattern_ref, counts_ref, list_sem, block_sem, piece_sem = refs[n_ctx + n_head :]
    lists = [
        pltpu.make_async_copy(pattern_hbm, pattern_ref, list_sem.at[0]),
        pltpu.make_async_copy(counts_hbm, counts_ref, list_sem.at[1]),
    ]
    for copy in lists:
        copy.start()
    h, me = lax.axis_index("head"), lax.axis_index("ctx")
    q_cols, kv_cols = q_ref.shape[1] // n_head, kv_ref.shape[1] // n_head
    copies = []
    for m in range(n_head):
        peer = lax.bitwise_xor(h, m)
        for ref, cols, at, s in ((q_ref, q_cols, 0, 0), (kv_ref, kv_cols, q_cols, 1)):
            copy = pltpu.make_async_copy(
                ref.at[:, pl.ds(pl.multiple_of(peer * cols, cols), cols)],
                pieces[m].at[:, pl.ds(at, cols)],
                piece_sem.at[m, s],
            )
            copy.start()
            copies.append(copy)
    for copy in lists:
        copy.wait()
    block = blocks[0].shape[0]
    shard_blocks = cache_ref.shape[1] // block
    for k in range(n_ctx):
        row = lax.rem(me + k, n_ctx)
        index = wanted_index(pattern_ref, counts_ref, row, me, shard_blocks)
        start = pl.multiple_of(index * block, block)
        copy = pltpu.make_async_copy(cache_ref.at[0, pl.ds(start, block), :], blocks[k], block_sem.at[k])
        copy.start()
        copies.append(copy)
    for i in range(pattern_ref.shape[0]):
        away = lax.rem(me - pattern_ref[i, me] // shard_blocks + n_ctx, n_ctx)
        away = jnp.where(i < counts_ref[me], away, UNUSED)
        slots_ref[i : i + 1, :] = jnp.full((1, slots_ref.shape[1]), away, jnp.int32)
    for copy in copies:
        copy.wait()


def attend_kernel(n_ctx, n_head, d, mine, slots_ref, *refs):
    outs = refs[len(refs) - len(mine) :]
    named = dict(zip(FEED + (("ctx", 0), ("head", 0)), refs))
    blocks = [named["ctx", k] for k in range(n_ctx)]
    pieces = [named["head", m] for m in range(n_head)]
    h = lax.axis_index("head")
    rows = pieces[0].shape[0]
    q_cols = pieces[0].shape[1] - 2 * d
    group = q_cols // d
    width, lanes = slots_ref.shape
    block = blocks[0].shape[0]
    keys, values, slot_bias = [], [], []
    for i in range(width):
        away = slots_ref[i : i + 1, :]
        kv = blocks[0][...]
        for k in range(1, n_ctx):
            kv = jnp.where(away == k, blocks[k][...], kv)
        keys.append(kv[:, :d])
        values.append(kv[:, d:])
        slot_bias.append(jnp.where(away[:, :block] == UNUSED, -jnp.inf, 0.0).astype(jnp.float32))
    for m in range(n_head):
        keys.append(pieces[m][:, q_cols : q_cols + d])
        values.append(pieces[m][:, q_cols + d :])
    keys, values = jnp.concatenate(keys, axis=0), jnp.concatenate(values, axis=0)
    span = n_head * rows
    column = lax.broadcasted_iota(jnp.int32, (rows, span), 1)
    row = lax.broadcasted_iota(jnp.int32, (rows, span), 0)
    key_token = lax.bitwise_xor(column // rows, h) * rows + column % rows
    rate = LOG2E / math.sqrt(d)
    for m, out in zip(mine, outs):
        q = jnp.concatenate([pieces[m][:, j * d : (j + 1) * d] for j in range(group)], axis=0)
        s = lax.dot_general(q, keys, (((1,), (1,)), ((), ())), preferred_element_type=jnp.float32)
        causal = jnp.where(lax.bitwise_xor(h, m) * rows + row >= key_token, 0.0, -jnp.inf)
        own = s[:, width * block :].reshape(group, rows, span) + causal[None]
        parts = [s[:, i * block : (i + 1) * block] + slot_bias[i] for i in range(width)]
        s = jnp.concatenate(parts + [own.reshape(group * rows, span)], axis=1)
        top = jnp.max(s, axis=1, keepdims=True)
        p = jnp.exp2((s - top) * rate)
        denom = jnp.sum(p, axis=1, keepdims=True)
        o = lax.dot_general(
            p.astype(jnp.bfloat16), values, (((1,), (0,)), ((), ())), preferred_element_type=jnp.float32
        )
        o = (o / denom).astype(jnp.bfloat16)
        for j in range(group):
            out[:, j * d : (j + 1) * d] = o[j * rows : (j + 1) * rows]


def join_kernel(n_head, *refs):
    out, sem = refs[n_head], refs[n_head + 1]
    order = [m for mine in STAGES for m in mine]
    pieces = [refs[order.index(m)] for m in range(n_head)]
    h = lax.axis_index("head")
    cols = pieces[0].shape[1]
    copies = []
    for m in range(n_head):
        start = pl.multiple_of(lax.bitwise_xor(h, m) * cols, cols)
        copy = pltpu.make_async_copy(pieces[m], out.at[:, pl.ds(start, cols)], sem.at[m])
        copy.start()
        copies.append(copy)
    for copy in copies:
        copy.wait()


def direct(n_ctx, n_head, queries, span_key_value, cache, pattern, counts):
    rows, d = queries.shape[0], cache.shape[2] // 2
    block = rows * n_head
    q_cols, kv_cols = queries.shape[1] // n_head, span_key_value.shape[1] // n_head
    bf16 = jnp.bfloat16
    around = [[(i, (i + k) % n_ctx) for i in range(n_ctx)] for k in range(n_ctx)]
    across = [[(i, i ^ m) for i in range(n_head)] for m in range(n_head)]

    prepared = pl.pallas_call(
        functools.partial(prepare_kernel, n_ctx, n_head),
        out_shape=[pltpu.VMEM((block, 2 * d), bf16)] * n_ctx
        + [pltpu.VMEM((rows, q_cols + kv_cols), bf16)] * n_head
        + [pltpu.VMEM((pattern.shape[1], 2 * d), jnp.int32)],
        in_specs=[ANY] * 5,
        out_specs=[VMEM] * (n_ctx + n_head + 1),
        scratch_shapes=[
            pltpu.SMEM(pattern.shape[::-1], jnp.int32),
            pltpu.SMEM(counts.shape, jnp.int32),
            pltpu.SemaphoreType.DMA((2,)),
            pltpu.SemaphoreType.DMA((n_ctx,)),
            pltpu.SemaphoreType.DMA((n_head, 2)),
        ],
        name="prepare",
    )(pattern.T, counts, cache, queries, span_key_value)
    blocks, pieces = list(prepared[:n_ctx]), list(prepared[n_ctx:-1])
    for axis, k in FEED:
        if axis == "ctx":
            blocks[k] = lax.ppermute(blocks[k], axis, around[k])
        else:
            pieces[k] = lax.ppermute(pieces[k], axis, across[k])
    held = {"ctx": blocks, "head": pieces}
    order = FEED + (("ctx", 0), ("head", 0))
    operands = [vmem(held[axis][k]) for axis, k in order]
    outs, last = [None] * n_head, []
    for mine in STAGES:
        made = pl.pallas_call(
            functools.partial(attend_kernel, n_ctx, n_head, d, mine),
            out_shape=[pltpu.VMEM((rows, q_cols), bf16)] * len(mine),
            in_specs=[VMEM] * (1 + n_ctx + n_head + len(last)),
            out_specs=[VMEM] * len(mine),
            name=f"attend{mine[0]}",
        )(vmem(prepared[-1]), *operands, *last)
        last = [vmem(made[0])]
        for m, x in zip(mine, made):
            outs[m] = lax.ppermute(x, "head", across[m]) if m else x
    return pl.pallas_call(
        functools.partial(join_kernel, n_head),
        out_shape=jax.ShapeDtypeStruct((rows, q_cols * n_head), bf16),
        in_specs=[VMEM] * n_head,
        out_specs=ANY,
        scratch_shapes=[pltpu.SemaphoreType.DMA((n_head,))],
        name="join",
    )(*[vmem(outs[m]) for mine in STAGES for m in mine])


def collect_kernel(n_ctx, block, pattern_ref, counts_ref, cache_ref, out_ref, sem):
    me = lax.axis_index("ctx")
    shard_blocks = cache_ref.shape[1] // block

    @pl.loop(0, n_ctx)
    def _(row):
        index = wanted_index(pattern_ref, counts_ref, row, me, shard_blocks)
        start = pl.multiple_of(index * block, block)
        copy = pltpu.make_async_copy(cache_ref.at[0, pl.ds(start, block), :], out_ref.at[row], sem)
        copy.start()
        copy.wait()


def slots_kernel(shard_blocks, pattern_ref, in_ref, out_ref, sem):
    me = lax.axis_index("ctx")

    @pl.loop(0, pattern_ref.shape[0])
    def _(i):
        copy = pltpu.make_async_copy(in_ref.at[pattern_ref[i, me] // shard_blocks], out_ref.at[i], sem)
        copy.start()
        copy.wait()


def absorb(carried, q, kv, allowed, scale):
    running_max, denom, weighted = carried
    d = q.shape[-1]
    scores = jnp.einsum("tjd,kd->jtk", q, kv[:, :d], preferred_element_type=jnp.float32) * scale
    masked = jnp.where(allowed, scores, -jnp.inf)
    new_max = jnp.maximum(running_max, jnp.max(masked, axis=-1))
    factor = jnp.exp(running_max - new_max)
    weights = jnp.where(allowed, jnp.exp(scores - new_max[..., None]), 0.0)
    denom = denom * factor + jnp.sum(weights, axis=-1)
    weighted = weighted * factor[..., None] + jnp.einsum(
        "jtk,kd->jtd", weights.astype(jnp.bfloat16), kv[:, d:], preferred_element_type=jnp.float32
    )
    return new_max, denom, weighted


def general(n_ctx, n_head, queries, span_key_value, cache, pattern, counts):
    d = cache.shape[2] // 2
    block = queries.shape[0] * n_head
    shard_blocks = cache.shape[1] // block
    width = pattern.shape[1]
    q = lax.all_to_all(queries, "head", split_axis=1, concat_axis=0, tiled=True)
    kv = lax.all_to_all(span_key_value, "head", split_axis=1, concat_axis=0, tiled=True)
    outgoing = pl.pallas_call(
        functools.partial(collect_kernel, n_ctx, block),
        out_shape=jax.ShapeDtypeStruct((n_ctx, block, 2 * d), jnp.bfloat16),
        in_specs=[SMEM, SMEM, ANY],
        out_specs=ANY,
        scratch_shapes=[pltpu.SemaphoreType.DMA],
        name="collect",
    )(pattern.T, counts, cache)
    incoming = lax.all_to_all(outgoing, "ctx", split_axis=0, concat_axis=0, tiled=True)
    slots = pl.pallas_call(
        functools.partial(slots_kernel, shard_blocks),
        out_shape=jax.ShapeDtypeStruct((width, block, 2 * d), jnp.bfloat16),
        in_specs=[SMEM, ANY],
        out_specs=ANY,
        scratch_shapes=[pltpu.SemaphoreType.DMA],
        name="slots",
    )(pattern.T, incoming)
    count = lax.dynamic_index_in_dim(counts, lax.axis_index("ctx"), 0, keepdims=False)
    group = q.shape[1] // d
    q = q.reshape(block, group, d)
    scale = 1.0 / math.sqrt(d)
    carried = (
        jnp.full((group, block), -jnp.inf, jnp.float32),
        jnp.zeros((group, block), jnp.float32),
        jnp.zeros((group, block, d), jnp.float32),
    )
    causal = jnp.arange(block)[:, None] >= jnp.arange(block)[None, :]
    carried = absorb(carried, q, kv, causal, scale)
    batch = math.gcd(width, 4)

    def step(at, carried):
        some = lax.dynamic_slice_in_dim(slots, at * batch, batch, 0).reshape(batch * block, 2 * d)
        usable = at * batch + jnp.arange(batch * block) // block < count
        return absorb(carried, q, some, usable, scale)

    _, denom, weighted = lax.fori_loop(0, width // batch, step, carried)
    result = (weighted / denom[..., None]).transpose(1, 0, 2).reshape(block, group * d)
    return lax.all_to_all(result.astype(jnp.bfloat16), "head", split_axis=0, concat_axis=1, tiled=True)


def solution(mesh):
    n_ctx, n_head = mesh.shape["ctx"], mesh.shape["head"]
    form = direct if n_ctx <= MAX_DIRECT else general
    return jax.shard_map(
        functools.partial(form, n_ctx, n_head),
        mesh=mesh,
        in_specs=(
            P(("grp", "ctx", "head"), None),
            P(("grp", "ctx", "head"), None),
            P("head", ("grp", "ctx"), None),
            P("grp", None),
            P("grp"),
        ),
        out_specs=P(("grp", "ctx", "head"), None),
        check_vma=False,
    )
```

```python
import functools
import math

import jax
import jax.numpy as jnp
from jax import lax
from jax.experimental import pallas as pl
from jax.experimental.pallas import tpu as pltpu
from jax.sharding import PartitionSpec as P

LOG2E = 1.4426950408889634
MAX_DIRECT = 4
UNUSED = 1 << 20
FEED = (("ctx", 1), ("ctx", 2), ("ctx", 3), ("head", 2), ("head", 3), ("head", 1))
TOGETHER = 4
STAGES = ((1, 2, 3, 0),)
ANY = pl.BlockSpec(memory_space=pl.ANY)
SMEM = pl.BlockSpec(memory_space=pltpu.SMEM)
VMEM = pl.BlockSpec(memory_space=pltpu.VMEM)


def vmem(x):
    return pltpu.with_memory_space_constraint(x, pltpu.VMEM)


def wanted_index(pattern_ref, counts_ref, row, owner, shard_blocks):
    def one(i, found):
        entry = pattern_ref[i, row]
        match = (i < counts_ref[row]) & (entry // shard_blocks == owner)
        return jnp.where(match, entry % shard_blocks, found)

    width = pattern_ref.shape[0]
    if width <= 4:
        found = jnp.int32(0)
        for i in range(width):
            found = one(i, found)
        return found
    return lax.fori_loop(0, width, one, jnp.int32(0))


def prepare_kernel(n_ctx, n_head, pattern_hbm, counts_hbm, cache_ref, q_ref, kv_ref, *refs):
    blocks, pieces = refs[:n_ctx], refs[n_ctx : n_ctx + n_head]
    slots_ref, pattern_ref, counts_ref, shard_ref, list_sem, shard_sem, piece_sem = refs[n_ctx + n_head :]
    lists = [
        pltpu.make_async_copy(pattern_hbm, pattern_ref, list_sem.at[0]),
        pltpu.make_async_copy(counts_hbm, counts_ref, list_sem.at[1]),
    ]
    shard = pltpu.make_async_copy(cache_ref.at[0], shard_ref, shard_sem)
    for copy in lists + [shard]:
        copy.start()
    h, me = lax.axis_index("head"), lax.axis_index("ctx")
    q_cols, kv_cols = q_ref.shape[1] // n_head, kv_ref.shape[1] // n_head
    copies = []
    for m in range(n_head):
        peer = lax.bitwise_xor(h, m)
        for ref, cols, at, s in ((q_ref, q_cols, 0, 0), (kv_ref, kv_cols, q_cols, 1)):
            copy = pltpu.make_async_copy(
                ref.at[:, pl.ds(pl.multiple_of(peer * cols, cols), cols)],
                pieces[m].at[:, pl.ds(at, cols)],
                piece_sem.at[m, s],
            )
            copy.start()
            copies.append(copy)
    for copy in lists:
        copy.wait()
    block = blocks[0].shape[0]
    shard_blocks = shard_ref.shape[0] // block
    starts = []
    for k in range(n_ctx):
        row = lax.rem(me + k, n_ctx)
        index = wanted_index(pattern_ref, counts_ref, row, me, shard_blocks)
        starts.append(pl.multiple_of(index * block, block))
    for i in range(pattern_ref.shape[0]):
        away = lax.rem(me - pattern_ref[i, me] // shard_blocks + n_ctx, n_ctx)
        away = jnp.where(i < counts_ref[me], away, UNUSED)
        slots_ref[i : i + 1, :] = jnp.full((1, slots_ref.shape[1]), away, jnp.int32)
    shard.wait()
    for k in range(n_ctx):
        blocks[k][...] = shard_ref[pl.ds(starts[k], block), :]
    for copy in copies:
        copy.wait()


def attend_kernel(n_ctx, n_head, d, mine, slots_ref, *refs):
    outs = refs[len(refs) - len(mine) :]
    named = dict(zip(FEED + (("ctx", 0), ("head", 0)), refs))
    blocks = [named["ctx", k] for k in range(n_ctx)]
    pieces = [named["head", m] for m in range(n_head)]
    h = lax.axis_index("head")
    rows = pieces[0].shape[0]
    q_cols = pieces[0].shape[1] - 2 * d
    group = q_cols // d
    width, lanes = slots_ref.shape
    block = blocks[0].shape[0]
    keys, values, slot_bias = [], [], []
    for i in range(width):
        away = slots_ref[i : i + 1, :]
        kv = blocks[0][...]
        for k in range(1, n_ctx):
            kv = jnp.where(away == k, blocks[k][...], kv)
        keys.append(kv[:, :d])
        values.append(kv[:, d:])
        slot_bias.append(jnp.where(away[:, :block] == UNUSED, -jnp.inf, 0.0).astype(jnp.float32))
    for m in range(n_head):
        keys.append(pieces[m][:, q_cols : q_cols + d])
        values.append(pieces[m][:, q_cols + d :])
    keys, values = jnp.concatenate(keys, axis=0), jnp.concatenate(values, axis=0)
    span = n_head * rows
    column = lax.broadcasted_iota(jnp.int32, (rows, span), 1)
    row = lax.broadcasted_iota(jnp.int32, (rows, span), 0)
    key_token = lax.bitwise_xor(column // rows, h) * rows + column % rows
    rate = LOG2E / math.sqrt(d)
    for first in range(0, len(mine), TOGETHER):
        some = mine[first : first + TOGETHER]
        q = jnp.concatenate(
            [pieces[m][:, j * d : (j + 1) * d] for m in some for j in range(group)], axis=0
        )
        s = lax.dot_general(q, keys, (((1,), (1,)), ((), ())), preferred_element_type=jnp.float32)
        causal = jnp.stack(
            [jnp.where(lax.bitwise_xor(h, m) * rows + row >= key_token, 0.0, -jnp.inf) for m in some]
        )
        own = s[:, width * block :].reshape(len(some), group, rows, span) + causal[:, None]
        parts = [s[:, i * block : (i + 1) * block] + slot_bias[i] for i in range(width)]
        s = jnp.concatenate(parts + [own.reshape(-1, span)], axis=1)
        top = jnp.max(s, axis=1, keepdims=True)
        p = jnp.exp2((s - top) * rate)
        denom = jnp.sum(p, axis=1, keepdims=True)
        o = lax.dot_general(
            p.astype(jnp.bfloat16), values, (((1,), (0,)), ((), ())), preferred_element_type=jnp.float32
        )
        o = (o / denom).astype(jnp.bfloat16)
        for n in range(len(some)):
            for j in range(group):
                at = (n * group + j) * rows
                outs[first + n][:, j * d : (j + 1) * d] = o[at : at + rows]


def join_kernel(n_head, *refs):
    out, sem = refs[n_head], refs[n_head + 1]
    order = [m for mine in STAGES for m in mine]
    pieces = [refs[order.index(m)] for m in range(n_head)]
    h = lax.axis_index("head")
    cols = pieces[0].shape[1]
    copies = []
    for m in range(n_head):
        start = pl.multiple_of(lax.bitwise_xor(h, m) * cols, cols)
        copy = pltpu.make_async_copy(pieces[m], out.at[:, pl.ds(start, cols)], sem.at[m])
        copy.start()
        copies.append(copy)
    for copy in copies:
        copy.wait()


def direct(n_ctx, n_head, queries, span_key_value, cache, pattern, counts):
    rows, d = queries.shape[0], cache.shape[2] // 2
    block = rows * n_head
    q_cols, kv_cols = queries.shape[1] // n_head, span_key_value.shape[1] // n_head
    bf16 = jnp.bfloat16
    around = [[(i, (i + k) % n_ctx) for i in range(n_ctx)] for k in range(n_ctx)]
    across = [[(i, i ^ m) for i in range(n_head)] for m in range(n_head)]

    prepared = pl.pallas_call(
        functools.partial(prepare_kernel, n_ctx, n_head),
        out_shape=[pltpu.VMEM((block, 2 * d), bf16)] * n_ctx
        + [pltpu.VMEM((rows, q_cols + kv_cols), bf16)] * n_head
        + [pltpu.VMEM((pattern.shape[1], 2 * d), jnp.int32)],
        in_specs=[ANY] * 5,
        out_specs=[VMEM] * (n_ctx + n_head + 1),
        scratch_shapes=[
            pltpu.SMEM(pattern.shape[::-1], jnp.int32),
            pltpu.SMEM(counts.shape, jnp.int32),
            pltpu.VMEM(cache.shape[1:], bf16),
            pltpu.SemaphoreType.DMA((2,)),
            pltpu.SemaphoreType.DMA,
            pltpu.SemaphoreType.DMA((n_head, 2)),
        ],
        name="prepare",
    )(pattern.T, counts, cache, queries, span_key_value)
    blocks, pieces = list(prepared[:n_ctx]), list(prepared[n_ctx:-1])
    for axis, k in FEED:
        if axis == "ctx":
            blocks[k] = lax.ppermute(blocks[k], axis, around[k])
        else:
            pieces[k] = lax.ppermute(pieces[k], axis, across[k])
    held = {"ctx": blocks, "head": pieces}
    order = FEED + (("ctx", 0), ("head", 0))
    operands = [vmem(held[axis][k]) for axis, k in order]
    outs, last = [None] * n_head, []
    for mine in STAGES:
        made = pl.pallas_call(
            functools.partial(attend_kernel, n_ctx, n_head, d, mine),
            out_shape=[pltpu.VMEM((rows, q_cols), bf16)] * len(mine),
            in_specs=[VMEM] * (1 + n_ctx + n_head + len(last)),
            out_specs=[VMEM] * len(mine),
            name=f"attend{mine[0]}",
        )(vmem(prepared[-1]), *operands, *last)
        last = [vmem(made[0])]
        for m, x in zip(mine, made):
            outs[m] = lax.ppermute(x, "head", across[m]) if m else x
    return pl.pallas_call(
        functools.partial(join_kernel, n_head),
        out_shape=jax.ShapeDtypeStruct((rows, q_cols * n_head), bf16),
        in_specs=[VMEM] * n_head,
        out_specs=ANY,
        scratch_shapes=[pltpu.SemaphoreType.DMA((n_head,))],
        name="join",
    )(*[vmem(outs[m]) for mine in STAGES for m in mine])


def collect_kernel(n_ctx, block, pattern_ref, counts_ref, cache_ref, out_ref, sem):
    me = lax.axis_index("ctx")
    shard_blocks = cache_ref.shape[1] // block

    @pl.loop(0, n_ctx)
    def _(row):
        index = wanted_index(pattern_ref, counts_ref, row, me, shard_blocks)
        start = pl.multiple_of(index * block, block)
        copy = pltpu.make_async_copy(cache_ref.at[0, pl.ds(start, block), :], out_ref.at[row], sem)
        copy.start()
        copy.wait()


def slots_kernel(shard_blocks, pattern_ref, in_ref, out_ref, sem):
    me = lax.axis_index("ctx")

    @pl.loop(0, pattern_ref.shape[0])
    def _(i):
        copy = pltpu.make_async_copy(in_ref.at[pattern_ref[i, me] // shard_blocks], out_ref.at[i], sem)
        copy.start()
        copy.wait()


def absorb(carried, q, kv, allowed, scale):
    running_max, denom, weighted = carried
    d = q.shape[-1]
    scores = jnp.einsum("tjd,kd->jtk", q, kv[:, :d], preferred_element_type=jnp.float32) * scale
    masked = jnp.where(allowed, scores, -jnp.inf)
    new_max = jnp.maximum(running_max, jnp.max(masked, axis=-1))
    factor = jnp.exp(running_max - new_max)
    weights = jnp.where(allowed, jnp.exp(scores - new_max[..., None]), 0.0)
    denom = denom * factor + jnp.sum(weights, axis=-1)
    weighted = weighted * factor[..., None] + jnp.einsum(
        "jtk,kd->jtd", weights.astype(jnp.bfloat16), kv[:, d:], preferred_element_type=jnp.float32
    )
    return new_max, denom, weighted


def general(n_ctx, n_head, queries, span_key_value, cache, pattern, counts):
    d = cache.shape[2] // 2
    block = queries.shape[0] * n_head
    shard_blocks = cache.shape[1] // block
    width = pattern.shape[1]
    q = lax.all_to_all(queries, "head", split_axis=1, concat_axis=0, tiled=True)
    kv = lax.all_to_all(span_key_value, "head", split_axis=1, concat_axis=0, tiled=True)
    outgoing = pl.pallas_call(
        functools.partial(collect_kernel, n_ctx, block),
        out_shape=jax.ShapeDtypeStruct((n_ctx, block, 2 * d), jnp.bfloat16),
        in_specs=[SMEM, SMEM, ANY],
        out_specs=ANY,
        scratch_shapes=[pltpu.SemaphoreType.DMA],
        name="collect",
    )(pattern.T, counts, cache)
    incoming = lax.all_to_all(outgoing, "ctx", split_axis=0, concat_axis=0, tiled=True)
    slots = pl.pallas_call(
        functools.partial(slots_kernel, shard_blocks),
        out_shape=jax.ShapeDtypeStruct((width, block, 2 * d), jnp.bfloat16),
        in_specs=[SMEM, ANY],
        out_specs=ANY,
        scratch_shapes=[pltpu.SemaphoreType.DMA],
        name="slots",
    )(pattern.T, incoming)
    count = lax.dynamic_index_in_dim(counts, lax.axis_index("ctx"), 0, keepdims=False)
    group = q.shape[1] // d
    q = q.reshape(block, group, d)
    scale = 1.0 / math.sqrt(d)
    carried = (
        jnp.full((group, block), -jnp.inf, jnp.float32),
        jnp.zeros((group, block), jnp.float32),
        jnp.zeros((group, block, d), jnp.float32),
    )
    causal = jnp.arange(block)[:, None] >= jnp.arange(block)[None, :]
    carried = absorb(carried, q, kv, causal, scale)
    batch = math.gcd(width, 4)

    def step(at, carried):
        some = lax.dynamic_slice_in_dim(slots, at * batch, batch, 0).reshape(batch * block, 2 * d)
        usable = at * batch + jnp.arange(batch * block) // block < count
        return absorb(carried, q, some, usable, scale)

    _, denom, weighted = lax.fori_loop(0, width // batch, step, carried)
    result = (weighted / denom[..., None]).transpose(1, 0, 2).reshape(block, group * d)
    return lax.all_to_all(result.astype(jnp.bfloat16), "head", split_axis=0, concat_axis=1, tiled=True)


def solution(mesh):
    n_ctx, n_head = mesh.shape["ctx"], mesh.shape["head"]
    form = direct if n_ctx <= MAX_DIRECT else general
    return jax.shard_map(
        functools.partial(form, n_ctx, n_head),
        mesh=mesh,
        in_specs=(
            P(("grp", "ctx", "head"), None),
            P(("grp", "ctx", "head"), None),
            P("head", ("grp", "ctx"), None),
            P("grp", None),
            P("grp"),
        ),
        out_specs=P(("grp", "ctx", "head"), None),
        check_vma=False,
    )
```

```python
import functools
import math

import jax
import jax.numpy as jnp
from jax import lax
from jax.experimental import pallas as pl
from jax.experimental.pallas import tpu as pltpu
from jax.sharding import PartitionSpec as P

LOG2E = 1.4426950408889634
MAX_DIRECT = 4
UNUSED = 1 << 20
CHOOSE, GATHER, EARLY, MID = 10**8, 10**10, 10**10, 10**9
ANY = pl.BlockSpec(memory_space=pl.ANY)
SMEM = pl.BlockSpec(memory_space=pltpu.SMEM)
VMEM = pl.BlockSpec(memory_space=pltpu.VMEM)


def vmem(x):
    return pltpu.with_memory_space_constraint(x, pltpu.VMEM)


def wanted_index(pattern_ref, counts_ref, row, owner, shard_blocks):
    def one(i, found):
        entry = pattern_ref[i, row]
        match = (i < counts_ref[row]) & (entry // shard_blocks == owner)
        return jnp.where(match, entry % shard_blocks, found)

    width = pattern_ref.shape[0]
    if width <= 4:
        found = jnp.int32(0)
        for i in range(width):
            found = one(i, found)
        return found
    return lax.fori_loop(0, width, one, jnp.int32(0))


def prepare_kernel(n_ctx, pattern_hbm, counts_hbm, cache_ref, *refs):
    blocks = refs[:n_ctx]
    slots_ref, pattern_ref, counts_ref, shard_ref, list_sem, shard_sem = refs[n_ctx:]
    lists = [
        pltpu.make_async_copy(pattern_hbm, pattern_ref, list_sem.at[0]),
        pltpu.make_async_copy(counts_hbm, counts_ref, list_sem.at[1]),
    ]
    shard = pltpu.make_async_copy(cache_ref.at[0], shard_ref, shard_sem)
    for copy in lists + [shard]:
        copy.start()
    for copy in lists:
        copy.wait()
    me = lax.axis_index("ctx")
    block = blocks[0].shape[0]
    shard_blocks = shard_ref.shape[0] // block
    starts = []
    for k in range(n_ctx):
        row = lax.rem(me + k, n_ctx)
        index = wanted_index(pattern_ref, counts_ref, row, me, shard_blocks)
        starts.append(pl.multiple_of(index * block, block))
    for i in range(pattern_ref.shape[0]):
        away = lax.rem(me - pattern_ref[i, me] // shard_blocks + n_ctx, n_ctx)
        away = jnp.where(i < counts_ref[me], away, UNUSED)
        slots_ref[i : i + 1, :] = jnp.full((1, slots_ref.shape[1]), away, jnp.int32)
    shard.wait()
    for k in range(n_ctx):
        blocks[k][...] = shard_ref[pl.ds(starts[k], block), :]


def choose_kernel(n_ctx, slots_ref, *refs):
    blocks, chosen_ref = refs[:n_ctx], refs[n_ctx]
    block = blocks[0].shape[0]
    for i in range(slots_ref.shape[0]):
        away = slots_ref[i : i + 1, :]
        kv = blocks[0][...]
        for k in range(1, n_ctx):
            kv = jnp.where(away == k, blocks[k][...], kv)
        chosen_ref[i * block : (i + 1) * block, :] = kv


def gather_kernel(*refs):
    rows = refs[0].shape[0]
    for m, ref in enumerate(refs[:-1]):
        refs[-1][m * rows : (m + 1) * rows, :] = ref[...]


def attend(n_head, mine, slots_ref, q_ref, kv_ref, chosen):
    h = lax.axis_index("head")
    d = chosen[0].shape[1] // 2
    rows, q_cols, kv_cols = q_ref.shape[0], q_ref.shape[1] // n_head, kv_ref.shape[1] // n_head
    group, width = q_cols // d, slots_ref.shape[0]
    block = chosen[0].shape[0] // width
    span = n_head * rows
    column = lax.broadcasted_iota(jnp.int32, (rows, span), 1)
    row = lax.broadcasted_iota(jnp.int32, (rows, span), 0)
    key_token = lax.bitwise_xor(column // rows, h) * rows + column % rows
    causal = jnp.where(h * rows + row >= key_token, 0.0, -jnp.inf)
    slot_bias = [
        jnp.where(slots_ref[i : i + 1, :block] == UNUSED, -jnp.inf, 0.0).astype(jnp.float32)
        for i in range(width)
    ]
    rate = LOG2E / math.sqrt(d)
    found = []
    for m, chosen_ref in zip(mine, chosen):
        peer = lax.bitwise_xor(h, m)

        def columns(ref, base, at):
            return ref[:, pl.ds(pl.multiple_of(peer * base + at, d), d)]

        keys = jnp.concatenate([chosen_ref[:, :d], columns(kv_ref, kv_cols, 0)], axis=0)
        values = jnp.concatenate([chosen_ref[:, d:], columns(kv_ref, kv_cols, d)], axis=0)
        q = jnp.concatenate([columns(q_ref, q_cols, j * d) for j in range(group)], axis=0)
        s = lax.dot_general(q, keys, (((1,), (1,)), ((), ())), preferred_element_type=jnp.float32)
        own = s[:, width * block :].reshape(group, rows, span) + causal[None]
        parts = [s[:, i * block : (i + 1) * block] + slot_bias[i] for i in range(width)]
        s = jnp.concatenate(parts + [own.reshape(group * rows, span)], axis=1)
        top = jnp.max(s, axis=1, keepdims=True)
        p = jnp.exp2((s - top) * rate)
        denom = jnp.sum(p, axis=1, keepdims=True)
        o = lax.dot_general(
            p.astype(jnp.bfloat16), values, (((1,), (0,)), ((), ())), preferred_element_type=jnp.float32
        )
        o = (o / denom).astype(jnp.bfloat16)
        found.append([o[j * rows : (j + 1) * rows] for j in range(group)])
    return found


def early_kernel(n_head, mine, slots_ref, q_ref, kv_ref, *refs):
    chosen, outs = refs[: len(mine)], refs[len(mine) :]
    for out, parts in zip(outs, attend(n_head, mine, slots_ref, q_ref, kv_ref, chosen)):
        d = parts[0].shape[1]
        for j, part in enumerate(parts):
            out[:, j * d : (j + 1) * d] = part


def late_kernel(n_head, before, mine, slots_ref, q_ref, kv_ref, *refs):
    chosen, refs = refs[: len(mine)], refs[len(mine) :]
    done, out_ref, made_ref, sem = refs[: len(before)], *refs[len(before) :]
    h = lax.axis_index("head")
    cols = q_ref.shape[1] // n_head

    def send(m, ref):
        start = pl.multiple_of(lax.bitwise_xor(h, m) * cols, cols)
        copy = pltpu.make_async_copy(ref, out_ref.at[:, pl.ds(start, cols)], sem.at[m])
        copy.start()
        return copy

    copies = [send(m, ref) for m, ref in zip(before, done)]
    for n, (m, parts) in enumerate(zip(mine, attend(n_head, mine, slots_ref, q_ref, kv_ref, chosen))):
        d = parts[0].shape[1]
        for j, part in enumerate(parts):
            made_ref[n, :, j * d : (j + 1) * d] = part
        copies.append(send(m, made_ref.at[n]))
    for copy in copies:
        copy.wait()


def after_kernel(x_ref, first_ref, out_ref):
    pass


def cost(flops):
    return pl.CostEstimate(flops=flops, bytes_accessed=1 << 20, transcendentals=0)


def direct(n_ctx, n_head, queries, span_key_value, cache, pattern, counts):
    rows, d = queries.shape[0], cache.shape[2] // 2
    block = rows * n_head
    q_cols = queries.shape[1] // n_head
    width = pattern.shape[1]
    bf16 = jnp.bfloat16
    around = [[(i, (i + k) % n_ctx) for i in range(n_ctx)] for k in range(n_ctx)]
    across = [[(i, i ^ m) for i in range(n_head)] for m in range(n_head)]

    *blocks, slots = pl.pallas_call(
        functools.partial(prepare_kernel, n_ctx),
        out_shape=[pltpu.VMEM((block, 2 * d), bf16)] * n_ctx + [pltpu.VMEM((width, 2 * d), jnp.int32)],
        in_specs=[ANY] * 3,
        out_specs=[VMEM] * (n_ctx + 1),
        scratch_shapes=[
            pltpu.SMEM(pattern.shape[::-1], jnp.int32),
            pltpu.SMEM(counts.shape, jnp.int32),
            pltpu.VMEM(cache.shape[1:], bf16),
            pltpu.SemaphoreType.DMA((2,)),
            pltpu.SemaphoreType.DMA,
        ],
        name="prepare",
    )(pattern.T, counts, cache)
    for k in range(1, n_ctx):
        blocks[k] = lax.ppermute(blocks[k], "ctx", around[k])
    pieces = [span_key_value] * n_head
    for m in (2, 3, 1):
        pieces[m] = lax.ppermute(span_key_value, "head", across[m])
    slots = vmem(slots)
    chosen = [None] * n_head
    chosen[0] = pl.pallas_call(
        functools.partial(choose_kernel, n_ctx),
        out_shape=pltpu.VMEM((width * block, 2 * d), bf16),
        in_specs=[VMEM] * (1 + n_ctx),
        out_specs=VMEM,
        cost_estimate=cost(CHOOSE),
        name="choose",
    )(slots, *map(vmem, blocks))
    chosen[1] = lax.ppermute(chosen[0], "head", across[1])
    chosen[2] = lax.ppermute(chosen[0], "head", across[2])
    kv = pl.pallas_call(
        gather_kernel,
        out_shape=pltpu.VMEM((block, span_key_value.shape[1]), bf16),
        in_specs=[VMEM] * n_head,
        out_specs=VMEM,
        cost_estimate=cost(GATHER),
        name="gather",
    )(*map(vmem, pieces))
    given = [slots, vmem(queries), vmem(kv)]

    def stage(mine, name, flops):
        return pl.pallas_call(
            functools.partial(early_kernel, n_head, mine),
            out_shape=[pltpu.VMEM((rows, q_cols), bf16)] * len(mine),
            in_specs=[VMEM] * (3 + len(mine)),
            out_specs=[VMEM] * len(mine),
            cost_estimate=cost(flops),
            name=name,
        )(*given, *[vmem(chosen[m]) for m in mine])

    near = stage((0, 1), "early", EARLY)
    chosen[2] = pl.pallas_call(
        after_kernel,
        out_shape=pltpu.VMEM(chosen[2].shape, bf16),
        in_specs=[VMEM, VMEM],
        out_specs=VMEM,
        input_output_aliases={0: 0},
        name="after",
    )(vmem(chosen[2]), vmem(near[0]))
    chosen[3] = lax.ppermute(chosen[2], "head", across[1])
    across_x = stage((2,), "mid", MID)
    return pl.pallas_call(
        functools.partial(late_kernel, n_head, (0, 1, 2), (3,)),
        out_shape=jax.ShapeDtypeStruct(queries.shape, bf16),
        in_specs=[VMEM] * 7,
        out_specs=ANY,
        scratch_shapes=[pltpu.VMEM((1, rows, q_cols), bf16), pltpu.SemaphoreType.DMA((n_head,))],
        name="late",
    )(*given, vmem(chosen[3]), *map(vmem, [*near, *across_x]))


def collect_kernel(n_ctx, block, pattern_ref, counts_ref, cache_ref, out_ref, sem):
    me = lax.axis_index("ctx")
    shard_blocks = cache_ref.shape[1] // block

    @pl.loop(0, n_ctx)
    def _(row):
        index = wanted_index(pattern_ref, counts_ref, row, me, shard_blocks)
        start = pl.multiple_of(index * block, block)
        copy = pltpu.make_async_copy(cache_ref.at[0, pl.ds(start, block), :], out_ref.at[row], sem)
        copy.start()
        copy.wait()


def slots_kernel(shard_blocks, pattern_ref, in_ref, out_ref, sem):
    me = lax.axis_index("ctx")

    @pl.loop(0, pattern_ref.shape[0])
    def _(i):
        copy = pltpu.make_async_copy(in_ref.at[pattern_ref[i, me] // shard_blocks], out_ref.at[i], sem)
        copy.start()
        copy.wait()


def absorb(carried, q, kv, allowed, scale):
    running_max, denom, weighted = carried
    d = q.shape[-1]
    scores = jnp.einsum("tjd,kd->jtk", q, kv[:, :d], preferred_element_type=jnp.float32) * scale
    masked = jnp.where(allowed, scores, -jnp.inf)
    new_max = jnp.maximum(running_max, jnp.max(masked, axis=-1))
    factor = jnp.exp(running_max - new_max)
    weights = jnp.where(allowed, jnp.exp(scores - new_max[..., None]), 0.0)
    denom = denom * factor + jnp.sum(weights, axis=-1)
    weighted = weighted * factor[..., None] + jnp.einsum(
        "jtk,kd->jtd", weights.astype(jnp.bfloat16), kv[:, d:], preferred_element_type=jnp.float32
    )
    return new_max, denom, weighted


def general(n_ctx, n_head, queries, span_key_value, cache, pattern, counts):
    d = cache.shape[2] // 2
    block = queries.shape[0] * n_head
    shard_blocks = cache.shape[1] // block
    width = pattern.shape[1]
    q = lax.all_to_all(queries, "head", split_axis=1, concat_axis=0, tiled=True)
    kv = lax.all_to_all(span_key_value, "head", split_axis=1, concat_axis=0, tiled=True)
    outgoing = pl.pallas_call(
        functools.partial(collect_kernel, n_ctx, block),
        out_shape=jax.ShapeDtypeStruct((n_ctx, block, 2 * d), jnp.bfloat16),
        in_specs=[SMEM, SMEM, ANY],
        out_specs=ANY,
        scratch_shapes=[pltpu.SemaphoreType.DMA],
        name="collect",
    )(pattern.T, counts, cache)
    incoming = lax.all_to_all(outgoing, "ctx", split_axis=0, concat_axis=0, tiled=True)
    slots = pl.pallas_call(
        functools.partial(slots_kernel, shard_blocks),
        out_shape=jax.ShapeDtypeStruct((width, block, 2 * d), jnp.bfloat16),
        in_specs=[SMEM, ANY],
        out_specs=ANY,
        scratch_shapes=[pltpu.SemaphoreType.DMA],
        name="slots",
    )(pattern.T, incoming)
    count = lax.dynamic_index_in_dim(counts, lax.axis_index("ctx"), 0, keepdims=False)
    group = q.shape[1] // d
    q = q.reshape(block, group, d)
    scale = 1.0 / math.sqrt(d)
    carried = (
        jnp.full((group, block), -jnp.inf, jnp.float32),
        jnp.zeros((group, block), jnp.float32),
        jnp.zeros((group, block, d), jnp.float32),
    )
    causal = jnp.arange(block)[:, None] >= jnp.arange(block)[None, :]
    carried = absorb(carried, q, kv, causal, scale)
    batch = math.gcd(width, 4)

    def step(at, carried):
        some = lax.dynamic_slice_in_dim(slots, at * batch, batch, 0).reshape(batch * block, 2 * d)
        usable = at * batch + jnp.arange(batch * block) // block < count
        return absorb(carried, q, some, usable, scale)

    _, denom, weighted = lax.fori_loop(0, width // batch, step, carried)
    result = (weighted / denom[..., None]).transpose(1, 0, 2).reshape(block, group * d)
    return lax.all_to_all(result.astype(jnp.bfloat16), "head", split_axis=0, concat_axis=1, tiled=True)


def solution(mesh):
    n_ctx, n_head = mesh.shape["ctx"], mesh.shape["head"]
    form = direct if n_ctx <= MAX_DIRECT else general
    return jax.shard_map(
        functools.partial(form, n_ctx, n_head),
        mesh=mesh,
        in_specs=(
            P(("grp", "ctx", "head"), None),
            P(("grp", "ctx", "head"), None),
            P("head", ("grp", "ctx"), None),
            P("grp", None),
            P("grp"),
        ),
        out_specs=P(("grp", "ctx", "head"), None),
        check_vma=False,
    )
```

```python
import functools
import math

import jax
import jax.numpy as jnp
from jax import lax
from jax.experimental import pallas as pl
from jax.experimental.pallas import tpu as pltpu
from jax.sharding import PartitionSpec as P

LOG2E = 1.4426950408889634
MAX_DIRECT = 4
UNUSED = 1 << 20
CHOOSE, GATHER, EARLY, MID = 10**7, 10**8, 10**9, 10**8
ANY = pl.BlockSpec(memory_space=pl.ANY)
SMEM = pl.BlockSpec(memory_space=pltpu.SMEM)
VMEM = pl.BlockSpec(memory_space=pltpu.VMEM)


def vmem(x):
    return pltpu.with_memory_space_constraint(x, pltpu.VMEM)


def wanted_index(pattern_ref, counts_ref, row, owner, shard_blocks):
    def one(i, found):
        entry = pattern_ref[i, row]
        match = (i < counts_ref[row]) & (entry // shard_blocks == owner)
        return jnp.where(match, entry % shard_blocks, found)

    width = pattern_ref.shape[0]
    if width <= 4:
        found = jnp.int32(0)
        for i in range(width):
            found = one(i, found)
        return found
    return lax.fori_loop(0, width, one, jnp.int32(0))


def prepare_kernel(n_ctx, pattern_hbm, counts_hbm, cache_ref, *refs):
    blocks = refs[:n_ctx]
    slots_ref, pattern_ref, counts_ref, shard_ref, list_sem, shard_sem = refs[n_ctx:]
    lists = [
        pltpu.make_async_copy(pattern_hbm, pattern_ref, list_sem.at[0]),
        pltpu.make_async_copy(counts_hbm, counts_ref, list_sem.at[1]),
    ]
    shard = pltpu.make_async_copy(cache_ref.at[0], shard_ref, shard_sem)
    for copy in lists + [shard]:
        copy.start()
    for copy in lists:
        copy.wait()
    me = lax.axis_index("ctx")
    block = blocks[0].shape[0]
    shard_blocks = shard_ref.shape[0] // block
    starts = []
    for k in range(n_ctx):
        row = lax.rem(me + k, n_ctx)
        index = wanted_index(pattern_ref, counts_ref, row, me, shard_blocks)
        starts.append(pl.multiple_of(index * block, block))
    for i in range(pattern_ref.shape[0]):
        away = lax.rem(me - pattern_ref[i, me] // shard_blocks + n_ctx, n_ctx)
        away = jnp.where(i < counts_ref[me], away, UNUSED)
        slots_ref[i : i + 1, :] = jnp.full((1, slots_ref.shape[1]), away, jnp.int32)
    shard.wait()
    for k in range(n_ctx):
        blocks[k][...] = shard_ref[pl.ds(starts[k], block), :]


def choose_kernel(n_ctx, slots_ref, *refs):
    blocks, chosen_ref = refs[:n_ctx], refs[n_ctx]
    block = blocks[0].shape[0]
    for i in range(slots_ref.shape[0]):
        away = slots_ref[i : i + 1, :]
        kv = blocks[0][...]
        for k in range(1, n_ctx):
            kv = jnp.where(away == k, blocks[k][...], kv)
        chosen_ref[i * block : (i + 1) * block, :] = kv


def gather_kernel(*refs):
    rows = refs[0].shape[0]
    for m, ref in enumerate(refs[:-1]):
        refs[-1][m * rows : (m + 1) * rows, :] = ref[...]


def attend(n_head, mine, slots_ref, q_ref, kv_ref, chosen):
    h = lax.axis_index("head")
    d = chosen[0].shape[1] // 2
    rows, q_cols, kv_cols = q_ref.shape[0], q_ref.shape[1] // n_head, kv_ref.shape[1] // n_head
    group, width = q_cols // d, slots_ref.shape[0]
    block = chosen[0].shape[0] // width
    span = n_head * rows
    column = lax.broadcasted_iota(jnp.int32, (rows, span), 1)
    row = lax.broadcasted_iota(jnp.int32, (rows, span), 0)
    key_token = lax.bitwise_xor(column // rows, h) * rows + column % rows
    causal = jnp.where(h * rows + row >= key_token, 0.0, -jnp.inf)
    slot_bias = [
        jnp.where(slots_ref[i : i + 1, :block] == UNUSED, -jnp.inf, 0.0).astype(jnp.float32)
        for i in range(width)
    ]
    rate = LOG2E / math.sqrt(d)
    found = []
    for m, chosen_ref in zip(mine, chosen):
        peer = lax.bitwise_xor(h, m)

        def columns(ref, base, at):
            return ref[:, pl.ds(pl.multiple_of(peer * base + at, d), d)]

        keys = jnp.concatenate([chosen_ref[:, :d], columns(kv_ref, kv_cols, 0)], axis=0)
        values = jnp.concatenate([chosen_ref[:, d:], columns(kv_ref, kv_cols, d)], axis=0)
        q = jnp.concatenate([columns(q_ref, q_cols, j * d) for j in range(group)], axis=0)
        s = lax.dot_general(q, keys, (((1,), (1,)), ((), ())), preferred_element_type=jnp.float32)
        own = s[:, width * block :].reshape(group, rows, span) + causal[None]
        parts = [s[:, i * block : (i + 1) * block] + slot_bias[i] for i in range(width)]
        s = jnp.concatenate(parts + [own.reshape(group * rows, span)], axis=1)
        top = jnp.max(s, axis=1, keepdims=True)
        p = jnp.exp2((s - top) * rate)
        denom = jnp.sum(p, axis=1, keepdims=True)
        o = lax.dot_general(
            p.astype(jnp.bfloat16), values, (((1,), (0,)), ((), ())), preferred_element_type=jnp.float32
        )
        o = (o / denom).astype(jnp.bfloat16)
        found.append([o[j * rows : (j + 1) * rows] for j in range(group)])
    return found


def early_kernel(n_head, mine, slots_ref, q_ref, kv_ref, *refs):
    chosen, outs = refs[: len(mine)], refs[len(mine) :]
    for out, parts in zip(outs, attend(n_head, mine, slots_ref, q_ref, kv_ref, chosen)):
        d = parts[0].shape[1]
        for j, part in enumerate(parts):
            out[:, j * d : (j + 1) * d] = part


def late_kernel(n_head, before, mine, slots_ref, q_ref, kv_ref, *refs):
    chosen, refs = refs[: len(mine)], refs[len(mine) :]
    done, out_ref, made_ref, sem = refs[: len(before)], *refs[len(before) :]
    h = lax.axis_index("head")
    cols = q_ref.shape[1] // n_head

    def send(m, ref):
        start = pl.multiple_of(lax.bitwise_xor(h, m) * cols, cols)
        copy = pltpu.make_async_copy(ref, out_ref.at[:, pl.ds(start, cols)], sem.at[m])
        copy.start()
        return copy

    copies = [send(m, ref) for m, ref in zip(before, done)]
    for n, (m, parts) in enumerate(zip(mine, attend(n_head, mine, slots_ref, q_ref, kv_ref, chosen))):
        d = parts[0].shape[1]
        for j, part in enumerate(parts):
            made_ref[n, :, j * d : (j + 1) * d] = part
        copies.append(send(m, made_ref.at[n]))
    for copy in copies:
        copy.wait()


def after_kernel(x_ref, first_ref, out_ref):
    pass


def cost(flops):
    return pl.CostEstimate(flops=flops, bytes_accessed=1 << 20, transcendentals=0)


def direct(n_ctx, n_head, queries, span_key_value, cache, pattern, counts):
    rows, d = queries.shape[0], cache.shape[2] // 2
    block = rows * n_head
    q_cols = queries.shape[1] // n_head
    width = pattern.shape[1]
    bf16 = jnp.bfloat16
    around = [[(i, (i + k) % n_ctx) for i in range(n_ctx)] for k in range(n_ctx)]
    across = [[(i, i ^ m) for i in range(n_head)] for m in range(n_head)]

    *blocks, slots = pl.pallas_call(
        functools.partial(prepare_kernel, n_ctx),
        out_shape=[pltpu.VMEM((block, 2 * d), bf16)] * n_ctx + [pltpu.VMEM((width, 2 * d), jnp.int32)],
        in_specs=[ANY] * 3,
        out_specs=[VMEM] * (n_ctx + 1),
        scratch_shapes=[
            pltpu.SMEM(pattern.shape[::-1], jnp.int32),
            pltpu.SMEM(counts.shape, jnp.int32),
            pltpu.VMEM(cache.shape[1:], bf16),
            pltpu.SemaphoreType.DMA((2,)),
            pltpu.SemaphoreType.DMA,
        ],
        name="prepare",
    )(pattern.T, counts, cache)
    for k in range(1, n_ctx):
        blocks[k] = lax.ppermute(blocks[k], "ctx", around[k])
    pieces = [span_key_value] * n_head
    for m in (2, 3, 1):
        pieces[m] = lax.ppermute(span_key_value, "head", across[m])
    slots = vmem(slots)
    chosen = [None] * n_head
    chosen[0] = pl.pallas_call(
        functools.partial(choose_kernel, n_ctx),
        out_shape=pltpu.VMEM((width * block, 2 * d), bf16),
        in_specs=[VMEM] * (1 + n_ctx),
        out_specs=VMEM,
        cost_estimate=cost(CHOOSE),
        name="choose",
    )(slots, *map(vmem, blocks))
    chosen[1] = lax.ppermute(chosen[0], "head", across[1])
    chosen[2] = lax.ppermute(chosen[0], "head", across[2])
    kv = pl.pallas_call(
        gather_kernel,
        out_shape=pltpu.VMEM((block, span_key_value.shape[1]), bf16),
        in_specs=[VMEM] * n_head,
        out_specs=VMEM,
        cost_estimate=cost(GATHER),
        name="gather",
    )(*map(vmem, pieces))
    given = [slots, vmem(queries), vmem(kv)]

    def stage(mine, name, flops):
        return pl.pallas_call(
            functools.partial(early_kernel, n_head, mine),
            out_shape=[pltpu.VMEM((rows, q_cols), bf16)] * len(mine),
            in_specs=[VMEM] * (3 + len(mine)),
            out_specs=[VMEM] * len(mine),
            cost_estimate=cost(flops),
            name=name,
        )(*given, *[vmem(chosen[m]) for m in mine])

    (own,) = stage((0,), "early", EARLY)
    chosen[2] = pl.pallas_call(
        after_kernel,
        out_shape=pltpu.VMEM(chosen[2].shape, bf16),
        in_specs=[VMEM, VMEM],
        out_specs=VMEM,
        input_output_aliases={0: 0},
        name="after",
    )(vmem(chosen[2]), vmem(own))
    chosen[3] = lax.ppermute(chosen[2], "head", across[1])
    middle = stage((1, 2), "mid", MID)
    return pl.pallas_call(
        functools.partial(late_kernel, n_head, (0, 1, 2), (3,)),
        out_shape=jax.ShapeDtypeStruct(queries.shape, bf16),
        in_specs=[VMEM] * 7,
        out_specs=ANY,
        scratch_shapes=[pltpu.VMEM((1, rows, q_cols), bf16), pltpu.SemaphoreType.DMA((n_head,))],
        name="late",
    )(*given, vmem(chosen[3]), *map(vmem, [own, *middle]))


def collect_kernel(n_ctx, block, pattern_ref, counts_ref, cache_ref, out_ref, sem):
    me = lax.axis_index("ctx")
    shard_blocks = cache_ref.shape[1] // block

    @pl.loop(0, n_ctx)
    def _(row):
        index = wanted_index(pattern_ref, counts_ref, row, me, shard_blocks)
        start = pl.multiple_of(index * block, block)
        copy = pltpu.make_async_copy(cache_ref.at[0, pl.ds(start, block), :], out_ref.at[row], sem)
        copy.start()
        copy.wait()


def slots_kernel(shard_blocks, pattern_ref, in_ref, out_ref, sem):
    me = lax.axis_index("ctx")

    @pl.loop(0, pattern_ref.shape[0])
    def _(i):
        copy = pltpu.make_async_copy(in_ref.at[pattern_ref[i, me] // shard_blocks], out_ref.at[i], sem)
        copy.start()
        copy.wait()


def absorb(carried, q, kv, allowed, scale):
    running_max, denom, weighted = carried
    d = q.shape[-1]
    scores = jnp.einsum("tjd,kd->jtk", q, kv[:, :d], preferred_element_type=jnp.float32) * scale
    masked = jnp.where(allowed, scores, -jnp.inf)
    new_max = jnp.maximum(running_max, jnp.max(masked, axis=-1))
    factor = jnp.exp(running_max - new_max)
    weights = jnp.where(allowed, jnp.exp(scores - new_max[..., None]), 0.0)
    denom = denom * factor + jnp.sum(weights, axis=-1)
    weighted = weighted * factor[..., None] + jnp.einsum(
        "jtk,kd->jtd", weights.astype(jnp.bfloat16), kv[:, d:], preferred_element_type=jnp.float32
    )
    return new_max, denom, weighted


def general(n_ctx, n_head, queries, span_key_value, cache, pattern, counts):
    d = cache.shape[2] // 2
    block = queries.shape[0] * n_head
    shard_blocks = cache.shape[1] // block
    width = pattern.shape[1]
    q = lax.all_to_all(queries, "head", split_axis=1, concat_axis=0, tiled=True)
    kv = lax.all_to_all(span_key_value, "head", split_axis=1, concat_axis=0, tiled=True)
    outgoing = pl.pallas_call(
        functools.partial(collect_kernel, n_ctx, block),
        out_shape=jax.ShapeDtypeStruct((n_ctx, block, 2 * d), jnp.bfloat16),
        in_specs=[SMEM, SMEM, ANY],
        out_specs=ANY,
        scratch_shapes=[pltpu.SemaphoreType.DMA],
        name="collect",
    )(pattern.T, counts, cache)
    incoming = lax.all_to_all(outgoing, "ctx", split_axis=0, concat_axis=0, tiled=True)
    slots = pl.pallas_call(
        functools.partial(slots_kernel, shard_blocks),
        out_shape=jax.ShapeDtypeStruct((width, block, 2 * d), jnp.bfloat16),
        in_specs=[SMEM, ANY],
        out_specs=ANY,
        scratch_shapes=[pltpu.SemaphoreType.DMA],
        name="slots",
    )(pattern.T, incoming)
    count = lax.dynamic_index_in_dim(counts, lax.axis_index("ctx"), 0, keepdims=False)
    group = q.shape[1] // d
    q = q.reshape(block, group, d)
    scale = 1.0 / math.sqrt(d)
    carried = (
        jnp.full((group, block), -jnp.inf, jnp.float32),
        jnp.zeros((group, block), jnp.float32),
        jnp.zeros((group, block, d), jnp.float32),
    )
    causal = jnp.arange(block)[:, None] >= jnp.arange(block)[None, :]
    carried = absorb(carried, q, kv, causal, scale)
    batch = math.gcd(width, 4)

    def step(at, carried):
        some = lax.dynamic_slice_in_dim(slots, at * batch, batch, 0).reshape(batch * block, 2 * d)
        usable = at * batch + jnp.arange(batch * block) // block < count
        return absorb(carried, q, some, usable, scale)

    _, denom, weighted = lax.fori_loop(0, width // batch, step, carried)
    result = (weighted / denom[..., None]).transpose(1, 0, 2).reshape(block, group * d)
    return lax.all_to_all(result.astype(jnp.bfloat16), "head", split_axis=0, concat_axis=1, tiled=True)


def solution(mesh):
    n_ctx, n_head = mesh.shape["ctx"], mesh.shape["head"]
    form = direct if n_ctx <= MAX_DIRECT else general
    return jax.shard_map(
        functools.partial(form, n_ctx, n_head),
        mesh=mesh,
        in_specs=(
            P(("grp", "ctx", "head"), None),
            P(("grp", "ctx", "head"), None),
            P("head", ("grp", "ctx"), None),
            P("grp", None),
            P("grp"),
        ),
        out_specs=P(("grp", "ctx", "head"), None),
        check_vma=False,
    )
```

```python
import functools
import math

import jax
import jax.numpy as jnp
from jax import lax
from jax.experimental import pallas as pl
from jax.experimental.pallas import tpu as pltpu
from jax.sharding import PartitionSpec as P

LOG2E = 1.4426950408889634
MAX_DIRECT = 4
UNUSED = 1 << 20
CHOOSE, GATHER, EARLY, MID = 10**7, 10**8, 10**8, 10**8
ANY = pl.BlockSpec(memory_space=pl.ANY)
SMEM = pl.BlockSpec(memory_space=pltpu.SMEM)
VMEM = pl.BlockSpec(memory_space=pltpu.VMEM)


def vmem(x):
    return pltpu.with_memory_space_constraint(x, pltpu.VMEM)


def wanted_index(pattern_ref, counts_ref, row, owner, shard_blocks):
    def one(i, found):
        entry = pattern_ref[i, row]
        match = (i < counts_ref[row]) & (entry // shard_blocks == owner)
        return jnp.where(match, entry % shard_blocks, found)

    width = pattern_ref.shape[0]
    if width <= 4:
        found = jnp.int32(0)
        for i in range(width):
            found = one(i, found)
        return found
    return lax.fori_loop(0, width, one, jnp.int32(0))


def prepare_kernel(n_ctx, pattern_hbm, counts_hbm, cache_ref, *refs):
    blocks = refs[:n_ctx]
    slots_ref, pattern_ref, counts_ref, shard_ref, list_sem, shard_sem = refs[n_ctx:]
    lists = [
        pltpu.make_async_copy(pattern_hbm, pattern_ref, list_sem.at[0]),
        pltpu.make_async_copy(counts_hbm, counts_ref, list_sem.at[1]),
    ]
    shard = pltpu.make_async_copy(cache_ref.at[0], shard_ref, shard_sem)
    for copy in lists + [shard]:
        copy.start()
    for copy in lists:
        copy.wait()
    me = lax.axis_index("ctx")
    block = blocks[0].shape[0]
    shard_blocks = shard_ref.shape[0] // block
    starts = []
    for k in range(n_ctx):
        row = lax.rem(me + k, n_ctx)
        index = wanted_index(pattern_ref, counts_ref, row, me, shard_blocks)
        starts.append(pl.multiple_of(index * block, block))
    for i in range(pattern_ref.shape[0]):
        away = lax.rem(me - pattern_ref[i, me] // shard_blocks + n_ctx, n_ctx)
        away = jnp.where(i < counts_ref[me], away, UNUSED)
        slots_ref[i : i + 1, :] = jnp.full((1, slots_ref.shape[1]), away, jnp.int32)
    shard.wait()
    for k in range(n_ctx):
        blocks[k][...] = shard_ref[pl.ds(starts[k], block), :]


def choose_kernel(n_ctx, slots_ref, *refs):
    blocks, chosen_ref = refs[:n_ctx], refs[n_ctx]
    block = blocks[0].shape[0]
    for i in range(slots_ref.shape[0]):
        away = slots_ref[i : i + 1, :]
        kv = blocks[0][...]
        for k in range(1, n_ctx):
            kv = jnp.where(away == k, blocks[k][...], kv)
        chosen_ref[i * block : (i + 1) * block, :] = kv


def gather_kernel(*refs):
    rows = refs[0].shape[0]
    for m, ref in enumerate(refs[:-1]):
        refs[-1][m * rows : (m + 1) * rows, :] = ref[...]


def attend(n_head, mine, slots_ref, q_ref, kv_ref, chosen):
    h = lax.axis_index("head")
    d = chosen[0].shape[1] // 2
    rows, q_cols, kv_cols = q_ref.shape[0], q_ref.shape[1] // n_head, kv_ref.shape[1] // n_head
    group, width = q_cols // d, slots_ref.shape[0]
    block = chosen[0].shape[0] // width
    span = n_head * rows
    column = lax.broadcasted_iota(jnp.int32, (rows, span), 1)
    row = lax.broadcasted_iota(jnp.int32, (rows, span), 0)
    key_token = lax.bitwise_xor(column // rows, h) * rows + column % rows
    causal = jnp.where(h * rows + row >= key_token, 0.0, -jnp.inf)
    slot_bias = [
        jnp.where(slots_ref[i : i + 1, :block] == UNUSED, -jnp.inf, 0.0).astype(jnp.float32)
        for i in range(width)
    ]
    rate = LOG2E / math.sqrt(d)
    found = []
    for m, chosen_ref in zip(mine, chosen):
        peer = lax.bitwise_xor(h, m)

        def columns(ref, base, at):
            return ref[:, pl.ds(pl.multiple_of(peer * base + at, d), d)]

        keys = jnp.concatenate([chosen_ref[:, :d], columns(kv_ref, kv_cols, 0)], axis=0)
        values = jnp.concatenate([chosen_ref[:, d:], columns(kv_ref, kv_cols, d)], axis=0)
        q = jnp.concatenate([columns(q_ref, q_cols, j * d) for j in range(group)], axis=0)
        s = lax.dot_general(q, keys, (((1,), (1,)), ((), ())), preferred_element_type=jnp.float32)
        own = s[:, width * block :].reshape(group, rows, span) + causal[None]
        parts = [s[:, i * block : (i + 1) * block] + slot_bias[i] for i in range(width)]
        s = jnp.concatenate(parts + [own.reshape(group * rows, span)], axis=1)
        top = jnp.max(s, axis=1, keepdims=True)
        p = jnp.exp2((s - top) * rate)
        denom = jnp.sum(p, axis=1, keepdims=True)
        o = lax.dot_general(
            p.astype(jnp.bfloat16), values, (((1,), (0,)), ((), ())), preferred_element_type=jnp.float32
        )
        o = (o / denom).astype(jnp.bfloat16)
        found.append([o[j * rows : (j + 1) * rows] for j in range(group)])
    return found


def early_kernel(n_head, mine, slots_ref, q_ref, kv_ref, *refs):
    chosen, outs = refs[: len(mine)], refs[len(mine) :]
    for out, parts in zip(outs, attend(n_head, mine, slots_ref, q_ref, kv_ref, chosen)):
        d = parts[0].shape[1]
        for j, part in enumerate(parts):
            out[:, j * d : (j + 1) * d] = part


def late_kernel(n_head, before, mine, slots_ref, q_ref, kv_ref, *refs):
    chosen, refs = refs[: len(mine)], refs[len(mine) :]
    done, out_ref, made_ref, sem = refs[: len(before)], *refs[len(before) :]
    h = lax.axis_index("head")
    cols = q_ref.shape[1] // n_head

    def send(m, ref):
        start = pl.multiple_of(lax.bitwise_xor(h, m) * cols, cols)
        copy = pltpu.make_async_copy(ref, out_ref.at[:, pl.ds(start, cols)], sem.at[m])
        copy.start()
        return copy

    copies = [send(m, ref) for m, ref in zip(before, done)]
    for n, (m, parts) in enumerate(zip(mine, attend(n_head, mine, slots_ref, q_ref, kv_ref, chosen))):
        d = parts[0].shape[1]
        for j, part in enumerate(parts):
            made_ref[n, :, j * d : (j + 1) * d] = part
        copies.append(send(m, made_ref.at[n]))
    for copy in copies:
        copy.wait()


def after_kernel(x_ref, first_ref, out_ref):
    pass


def cost(flops):
    return pl.CostEstimate(flops=flops, bytes_accessed=1 << 20, transcendentals=0)


def direct(n_ctx, n_head, queries, span_key_value, cache, pattern, counts):
    rows, d = queries.shape[0], cache.shape[2] // 2
    block = rows * n_head
    q_cols = queries.shape[1] // n_head
    width = pattern.shape[1]
    bf16 = jnp.bfloat16
    around = [[(i, (i + k) % n_ctx) for i in range(n_ctx)] for k in range(n_ctx)]
    across = [[(i, i ^ m) for i in range(n_head)] for m in range(n_head)]

    *blocks, slots = pl.pallas_call(
        functools.partial(prepare_kernel, n_ctx),
        out_shape=[pltpu.VMEM((block, 2 * d), bf16)] * n_ctx + [pltpu.VMEM((width, 2 * d), jnp.int32)],
        in_specs=[ANY] * 3,
        out_specs=[VMEM] * (n_ctx + 1),
        scratch_shapes=[
            pltpu.SMEM(pattern.shape[::-1], jnp.int32),
            pltpu.SMEM(counts.shape, jnp.int32),
            pltpu.VMEM(cache.shape[1:], bf16),
            pltpu.SemaphoreType.DMA((2,)),
            pltpu.SemaphoreType.DMA,
        ],
        name="prepare",
    )(pattern.T, counts, cache)
    for k in range(1, n_ctx):
        blocks[k] = lax.ppermute(blocks[k], "ctx", around[k])
    pieces = [span_key_value] * n_head
    for m in (2, 1):
        pieces[m] = lax.ppermute(span_key_value, "head", across[m])
    pieces[3] = lax.ppermute(pieces[2], "head", across[1])
    slots = vmem(slots)
    chosen = [None] * n_head
    chosen[0] = pl.pallas_call(
        functools.partial(choose_kernel, n_ctx),
        out_shape=pltpu.VMEM((width * block, 2 * d), bf16),
        in_specs=[VMEM] * (1 + n_ctx),
        out_specs=VMEM,
        cost_estimate=cost(CHOOSE),
        name="choose",
    )(slots, *map(vmem, blocks))
    chosen[1] = lax.ppermute(chosen[0], "head", across[1])
    chosen[2] = lax.ppermute(chosen[0], "head", across[2])
    kv = pl.pallas_call(
        gather_kernel,
        out_shape=pltpu.VMEM((block, span_key_value.shape[1]), bf16),
        in_specs=[VMEM] * n_head,
        out_specs=VMEM,
        cost_estimate=cost(GATHER),
        name="gather",
    )(*map(vmem, pieces))
    given = [slots, vmem(queries), vmem(kv)]

    def stage(mine, name, flops):
        return pl.pallas_call(
            functools.partial(early_kernel, n_head, mine),
            out_shape=[pltpu.VMEM((rows, q_cols), bf16)] * len(mine),
            in_specs=[VMEM] * (3 + len(mine)),
            out_specs=[VMEM] * len(mine),
            cost_estimate=cost(flops),
            name=name,
        )(*given, *[vmem(chosen[m]) for m in mine])

    (own,) = stage((0,), "early", EARLY)
    chosen[2] = pl.pallas_call(
        after_kernel,
        out_shape=pltpu.VMEM(chosen[2].shape, bf16),
        in_specs=[VMEM, VMEM],
        out_specs=VMEM,
        input_output_aliases={0: 0},
        name="after",
    )(vmem(chosen[2]), vmem(own))
    chosen[3] = lax.ppermute(chosen[2], "head", across[1])
    middle = stage((1, 2), "mid", MID)
    return pl.pallas_call(
        functools.partial(late_kernel, n_head, (0, 1, 2), (3,)),
        out_shape=jax.ShapeDtypeStruct(queries.shape, bf16),
        in_specs=[VMEM] * 7,
        out_specs=ANY,
        scratch_shapes=[pltpu.VMEM((1, rows, q_cols), bf16), pltpu.SemaphoreType.DMA((n_head,))],
        name="late",
    )(*given, vmem(chosen[3]), *map(vmem, [own, *middle]))


def collect_kernel(n_ctx, block, pattern_ref, counts_ref, cache_ref, out_ref, sem):
    me = lax.axis_index("ctx")
    shard_blocks = cache_ref.shape[1] // block

    @pl.loop(0, n_ctx)
    def _(row):
        index = wanted_index(pattern_ref, counts_ref, row, me, shard_blocks)
        start = pl.multiple_of(index * block, block)
        copy = pltpu.make_async_copy(cache_ref.at[0, pl.ds(start, block), :], out_ref.at[row], sem)
        copy.start()
        copy.wait()


def slots_kernel(shard_blocks, pattern_ref, in_ref, out_ref, sem):
    me = lax.axis_index("ctx")

    @pl.loop(0, pattern_ref.shape[0])
    def _(i):
        copy = pltpu.make_async_copy(in_ref.at[pattern_ref[i, me] // shard_blocks], out_ref.at[i], sem)
        copy.start()
        copy.wait()


def absorb(carried, q, kv, allowed, scale):
    running_max, denom, weighted = carried
    d = q.shape[-1]
    scores = jnp.einsum("tjd,kd->jtk", q, kv[:, :d], preferred_element_type=jnp.float32) * scale
    masked = jnp.where(allowed, scores, -jnp.inf)
    new_max = jnp.maximum(running_max, jnp.max(masked, axis=-1))
    factor = jnp.exp(running_max - new_max)
    weights = jnp.where(allowed, jnp.exp(scores - new_max[..., None]), 0.0)
    denom = denom * factor + jnp.sum(weights, axis=-1)
    weighted = weighted * factor[..., None] + jnp.einsum(
        "jtk,kd->jtd", weights.astype(jnp.bfloat16), kv[:, d:], preferred_element_type=jnp.float32
    )
    return new_max, denom, weighted


def general(n_ctx, n_head, queries, span_key_value, cache, pattern, counts):
    d = cache.shape[2] // 2
    block = queries.shape[0] * n_head
    shard_blocks = cache.shape[1] // block
    width = pattern.shape[1]
    q = lax.all_to_all(queries, "head", split_axis=1, concat_axis=0, tiled=True)
    kv = lax.all_to_all(span_key_value, "head", split_axis=1, concat_axis=0, tiled=True)
    outgoing = pl.pallas_call(
        functools.partial(collect_kernel, n_ctx, block),
        out_shape=jax.ShapeDtypeStruct((n_ctx, block, 2 * d), jnp.bfloat16),
        in_specs=[SMEM, SMEM, ANY],
        out_specs=ANY,
        scratch_shapes=[pltpu.SemaphoreType.DMA],
        name="collect",
    )(pattern.T, counts, cache)
    incoming = lax.all_to_all(outgoing, "ctx", split_axis=0, concat_axis=0, tiled=True)
    slots = pl.pallas_call(
        functools.partial(slots_kernel, shard_blocks),
        out_shape=jax.ShapeDtypeStruct((width, block, 2 * d), jnp.bfloat16),
        in_specs=[SMEM, ANY],
        out_specs=ANY,
        scratch_shapes=[pltpu.SemaphoreType.DMA],
        name="slots",
    )(pattern.T, incoming)
    count = lax.dynamic_index_in_dim(counts, lax.axis_index("ctx"), 0, keepdims=False)
    group = q.shape[1] // d
    q = q.reshape(block, group, d)
    scale = 1.0 / math.sqrt(d)
    carried = (
        jnp.full((group, block), -jnp.inf, jnp.float32),
        jnp.zeros((group, block), jnp.float32),
        jnp.zeros((group, block, d), jnp.float32),
    )
    causal = jnp.arange(block)[:, None] >= jnp.arange(block)[None, :]
    carried = absorb(carried, q, kv, causal, scale)
    batch = math.gcd(width, 4)

    def step(at, carried):
        some = lax.dynamic_slice_in_dim(slots, at * batch, batch, 0).reshape(batch * block, 2 * d)
        usable = at * batch + jnp.arange(batch * block) // block < count
        return absorb(carried, q, some, usable, scale)

    _, denom, weighted = lax.fori_loop(0, width // batch, step, carried)
    result = (weighted / denom[..., None]).transpose(1, 0, 2).reshape(block, group * d)
    return lax.all_to_all(result.astype(jnp.bfloat16), "head", split_axis=0, concat_axis=1, tiled=True)


def solution(mesh):
    n_ctx, n_head = mesh.shape["ctx"], mesh.shape["head"]
    form = direct if n_ctx <= MAX_DIRECT else general
    return jax.shard_map(
        functools.partial(form, n_ctx, n_head),
        mesh=mesh,
        in_specs=(
            P(("grp", "ctx", "head"), None),
            P(("grp", "ctx", "head"), None),
            P("head", ("grp", "ctx"), None),
            P("grp", None),
            P("grp"),
        ),
        out_specs=P(("grp", "ctx", "head"), None),
        check_vma=False,
    )
```

```python
import functools
import math

import jax
import jax.numpy as jnp
from jax import lax
from jax.experimental import pallas as pl
from jax.experimental.pallas import tpu as pltpu
from jax.sharding import PartitionSpec as P

LOG2E = 1.4426950408889634
UNUSED = 1 << 20
CHOOSE, GATHER, EARLY, MID = 10**7, 10**8, 10**8, 10**8
ANY = pl.BlockSpec(memory_space=pl.ANY)
SMEM = pl.BlockSpec(memory_space=pltpu.SMEM)
VMEM = pl.BlockSpec(memory_space=pltpu.VMEM)


def vmem(x):
    return pltpu.with_memory_space_constraint(x, pltpu.VMEM)


def wanted_index(pattern_ref, counts_ref, row, owner, shard_blocks):
    def one(i, found):
        entry = pattern_ref[i, row]
        match = (i < counts_ref[row]) & (entry // shard_blocks == owner)
        return jnp.where(match, entry % shard_blocks, found)

    width = pattern_ref.shape[0]
    if width <= 4:
        found = jnp.int32(0)
        for i in range(width):
            found = one(i, found)
        return found
    return lax.fori_loop(0, width, one, jnp.int32(0))


def swap_ends(i):
    return i ^ (i >> 1)


def prepare_kernel(n_ctx, pattern_hbm, counts_hbm, cache_ref, *refs):
    blocks = refs[:n_ctx]
    slots_ref, pattern_ref, counts_ref, shard_ref, list_sem, shard_sem = refs[n_ctx:]
    lists = [
        pltpu.make_async_copy(pattern_hbm, pattern_ref, list_sem.at[0]),
        pltpu.make_async_copy(counts_hbm, counts_ref, list_sem.at[1]),
    ]
    shard = pltpu.make_async_copy(cache_ref.at[0], shard_ref, shard_sem)
    for copy in lists + [shard]:
        copy.start()
    for copy in lists:
        copy.wait()
    me = lax.axis_index("ctx")
    place = swap_ends(me)
    block = blocks[0].shape[0]
    shard_blocks = shard_ref.shape[0] // block
    starts = []
    for k in range(n_ctx):
        row = swap_ends(lax.rem(place + k, n_ctx))
        index = wanted_index(pattern_ref, counts_ref, row, me, shard_blocks)
        starts.append(pl.multiple_of(index * block, block))
    for i in range(pattern_ref.shape[0]):
        away = lax.rem(place - swap_ends(pattern_ref[i, me] // shard_blocks) + n_ctx, n_ctx)
        away = jnp.where(i < counts_ref[me], away, UNUSED)
        slots_ref[i : i + 1, :] = jnp.full((1, slots_ref.shape[1]), away, jnp.int32)
    shard.wait()
    for k in range(n_ctx):
        blocks[k][...] = shard_ref[pl.ds(starts[k], block), :]


def choose_kernel(n_ctx, slots_ref, *refs):
    blocks, chosen_ref = refs[:n_ctx], refs[n_ctx]
    block = blocks[0].shape[0]
    for i in range(slots_ref.shape[0]):
        away = slots_ref[i : i + 1, :]
        kv = blocks[0][...]
        for k in range(1, n_ctx):
            kv = jnp.where(away == k, blocks[k][...], kv)
        chosen_ref[i * block : (i + 1) * block, :] = kv


def gather_kernel(*refs):
    rows = refs[0].shape[0]
    for m, ref in enumerate(refs[:-1]):
        refs[-1][m * rows : (m + 1) * rows, :] = ref[...]


def attend(n_head, mine, slots_ref, q_ref, kv_ref, chosen):
    h = lax.axis_index("head")
    d = chosen[0].shape[1] // 2
    rows, q_cols, kv_cols = q_ref.shape[0], q_ref.shape[1] // n_head, kv_ref.shape[1] // n_head
    group, width = q_cols // d, slots_ref.shape[0]
    block = chosen[0].shape[0] // width
    span = n_head * rows
    column = lax.broadcasted_iota(jnp.int32, (rows, span), 1)
    row = lax.broadcasted_iota(jnp.int32, (rows, span), 0)
    key_token = lax.bitwise_xor(column // rows, h) * rows + column % rows
    causal = jnp.where(h * rows + row >= key_token, 0.0, -jnp.inf)
    slot_bias = [
        jnp.where(slots_ref[i : i + 1, :block] == UNUSED, -jnp.inf, 0.0).astype(jnp.float32)
        for i in range(width)
    ]
    rate = LOG2E / math.sqrt(d)
    found = []
    for m, chosen_ref in zip(mine, chosen):
        peer = lax.bitwise_xor(h, m)

        def columns(ref, base, at):
            return ref[:, pl.ds(pl.multiple_of(peer * base + at, d), d)]

        keys = jnp.concatenate([chosen_ref[:, :d], columns(kv_ref, kv_cols, 0)], axis=0)
        values = jnp.concatenate([chosen_ref[:, d:], columns(kv_ref, kv_cols, d)], axis=0)
        q = jnp.concatenate([columns(q_ref, q_cols, j * d) for j in range(group)], axis=0)
        s = lax.dot_general(q, keys, (((1,), (1,)), ((), ())), preferred_element_type=jnp.float32)
        own = s[:, width * block :].reshape(group, rows, span) + causal[None]
        parts = [s[:, i * block : (i + 1) * block] + slot_bias[i] for i in range(width)]
        s = jnp.concatenate(parts + [own.reshape(group * rows, span)], axis=1)
        top = jnp.max(s, axis=1, keepdims=True)
        p = jnp.exp2((s - top) * rate)
        denom = jnp.sum(p, axis=1, keepdims=True)
        o = lax.dot_general(
            p.astype(jnp.bfloat16), values, (((1,), (0,)), ((), ())), preferred_element_type=jnp.float32
        )
        o = (o / denom).astype(jnp.bfloat16)
        found.append([o[j * rows : (j + 1) * rows] for j in range(group)])
    return found


def early_kernel(n_head, mine, slots_ref, q_ref, kv_ref, *refs):
    chosen, outs = refs[: len(mine)], refs[len(mine) :]
    for out, parts in zip(outs, attend(n_head, mine, slots_ref, q_ref, kv_ref, chosen)):
        d = parts[0].shape[1]
        for j, part in enumerate(parts):
            out[:, j * d : (j + 1) * d] = part


def late_kernel(n_head, before, mine, slots_ref, q_ref, kv_ref, *refs):
    chosen, refs = refs[: len(mine)], refs[len(mine) :]
    done, out_ref, made_ref, sem = refs[: len(before)], *refs[len(before) :]
    h = lax.axis_index("head")
    cols = q_ref.shape[1] // n_head

    def send(m, ref):
        start = pl.multiple_of(lax.bitwise_xor(h, m) * cols, cols)
        copy = pltpu.make_async_copy(ref, out_ref.at[:, pl.ds(start, cols)], sem.at[m])
        copy.start()
        return copy

    copies = [send(m, ref) for m, ref in zip(before, done)]
    for n, (m, parts) in enumerate(zip(mine, attend(n_head, mine, slots_ref, q_ref, kv_ref, chosen))):
        d = parts[0].shape[1]
        for j, part in enumerate(parts):
            made_ref[n, :, j * d : (j + 1) * d] = part
        copies.append(send(m, made_ref.at[n]))
    for copy in copies:
        copy.wait()


def after_kernel(x_ref, first_ref, out_ref):
    pass


def cost(flops):
    return pl.CostEstimate(flops=flops, bytes_accessed=1 << 20, transcendentals=0)


def direct(n_ctx, n_head, queries, span_key_value, cache, pattern, counts):
    rows, d = queries.shape[0], cache.shape[2] // 2
    block = rows * n_head
    q_cols = queries.shape[1] // n_head
    width = pattern.shape[1]
    bf16 = jnp.bfloat16
    around = [
        [(swap_ends(i), swap_ends((i + k) % n_ctx)) for i in range(n_ctx)] for k in range(n_ctx)
    ]
    across = [[(i, i ^ m) for i in range(n_head)] for m in range(n_head)]

    *blocks, slots = pl.pallas_call(
        functools.partial(prepare_kernel, n_ctx),
        out_shape=[pltpu.VMEM((block, 2 * d), bf16)] * n_ctx + [pltpu.VMEM((width, 2 * d), jnp.int32)],
        in_specs=[ANY] * 3,
        out_specs=[VMEM] * (n_ctx + 1),
        scratch_shapes=[
            pltpu.SMEM(pattern.shape[::-1], jnp.int32),
            pltpu.SMEM(counts.shape, jnp.int32),
            pltpu.VMEM(cache.shape[1:], bf16),
            pltpu.SemaphoreType.DMA((2,)),
            pltpu.SemaphoreType.DMA,
        ],
        name="prepare",
    )(pattern.T, counts, cache)
    for k in range(1, n_ctx):
        blocks[k] = lax.ppermute(blocks[k], "ctx", around[k])
    pieces = [span_key_value] * n_head
    for m in (2, 1):
        pieces[m] = lax.ppermute(span_key_value, "head", across[m])
    pieces[3] = lax.ppermute(pieces[2], "head", across[1])
    slots = vmem(slots)
    chosen = [None] * n_head
    chosen[0] = pl.pallas_call(
        functools.partial(choose_kernel, n_ctx),
        out_shape=pltpu.VMEM((width * block, 2 * d), bf16),
        in_specs=[VMEM] * (1 + n_ctx),
        out_specs=VMEM,
        cost_estimate=cost(CHOOSE),
        name="choose",
    )(slots, *map(vmem, blocks))
    chosen[1] = lax.ppermute(chosen[0], "head", across[1])
    chosen[2] = lax.ppermute(chosen[0], "head", across[2])
    kv = pl.pallas_call(
        gather_kernel,
        out_shape=pltpu.VMEM((block, span_key_value.shape[1]), bf16),
        in_specs=[VMEM] * n_head,
        out_specs=VMEM,
        cost_estimate=cost(GATHER),
        name="gather",
    )(*map(vmem, pieces))
    given = [slots, vmem(queries), vmem(kv)]

    def stage(mine, name, flops):
        return pl.pallas_call(
            functools.partial(early_kernel, n_head, mine),
            out_shape=[pltpu.VMEM((rows, q_cols), bf16)] * len(mine),
            in_specs=[VMEM] * (3 + len(mine)),
            out_specs=[VMEM] * len(mine),
            cost_estimate=cost(flops),
            name=name,
        )(*given, *[vmem(chosen[m]) for m in mine])

    (own,) = stage((0,), "early", EARLY)
    chosen[2] = pl.pallas_call(
        after_kernel,
        out_shape=pltpu.VMEM(chosen[2].shape, bf16),
        in_specs=[VMEM, VMEM],
        out_specs=VMEM,
        input_output_aliases={0: 0},
        name="after",
    )(vmem(chosen[2]), vmem(own))
    chosen[3] = lax.ppermute(chosen[2], "head", across[1])
    middle = stage((1, 2), "mid", MID)
    return pl.pallas_call(
        functools.partial(late_kernel, n_head, (0, 1, 2), (3,)),
        out_shape=jax.ShapeDtypeStruct(queries.shape, bf16),
        in_specs=[VMEM] * 7,
        out_specs=ANY,
        scratch_shapes=[pltpu.VMEM((1, rows, q_cols), bf16), pltpu.SemaphoreType.DMA((n_head,))],
        name="late",
    )(*given, vmem(chosen[3]), *map(vmem, [own, *middle]))


def collect_kernel(n_ctx, block, pattern_ref, counts_ref, cache_ref, out_ref, sem):
    me = lax.axis_index("ctx")
    shard_blocks = cache_ref.shape[1] // block

    @pl.loop(0, n_ctx)
    def _(row):
        index = wanted_index(pattern_ref, counts_ref, row, me, shard_blocks)
        start = pl.multiple_of(index * block, block)
        copy = pltpu.make_async_copy(cache_ref.at[0, pl.ds(start, block), :], out_ref.at[row], sem)
        copy.start()
        copy.wait()


def slots_kernel(shard_blocks, pattern_ref, in_ref, out_ref, sem):
    me = lax.axis_index("ctx")

    @pl.loop(0, pattern_ref.shape[0])
    def _(i):
        copy = pltpu.make_async_copy(in_ref.at[pattern_ref[i, me] // shard_blocks], out_ref.at[i], sem)
        copy.start()
        copy.wait()


def absorb(carried, q, kv, allowed, scale):
    running_max, denom, weighted = carried
    d = q.shape[-1]
    scores = jnp.einsum("tjd,kd->jtk", q, kv[:, :d], preferred_element_type=jnp.float32) * scale
    masked = jnp.where(allowed, scores, -jnp.inf)
    new_max = jnp.maximum(running_max, jnp.max(masked, axis=-1))
    factor = jnp.exp(running_max - new_max)
    weights = jnp.where(allowed, jnp.exp(scores - new_max[..., None]), 0.0)
    denom = denom * factor + jnp.sum(weights, axis=-1)
    weighted = weighted * factor[..., None] + jnp.einsum(
        "jtk,kd->jtd", weights.astype(jnp.bfloat16), kv[:, d:], preferred_element_type=jnp.float32
    )
    return new_max, denom, weighted


def general(n_ctx, n_head, queries, span_key_value, cache, pattern, counts):
    d = cache.shape[2] // 2
    block = queries.shape[0] * n_head
    shard_blocks = cache.shape[1] // block
    width = pattern.shape[1]
    q = lax.all_to_all(queries, "head", split_axis=1, concat_axis=0, tiled=True)
    kv = lax.all_to_all(span_key_value, "head", split_axis=1, concat_axis=0, tiled=True)
    outgoing = pl.pallas_call(
        functools.partial(collect_kernel, n_ctx, block),
        out_shape=jax.ShapeDtypeStruct((n_ctx, block, 2 * d), jnp.bfloat16),
        in_specs=[SMEM, SMEM, ANY],
        out_specs=ANY,
        scratch_shapes=[pltpu.SemaphoreType.DMA],
        name="collect",
    )(pattern.T, counts, cache)
    incoming = lax.all_to_all(outgoing, "ctx", split_axis=0, concat_axis=0, tiled=True)
    slots = pl.pallas_call(
        functools.partial(slots_kernel, shard_blocks),
        out_shape=jax.ShapeDtypeStruct((width, block, 2 * d), jnp.bfloat16),
        in_specs=[SMEM, ANY],
        out_specs=ANY,
        scratch_shapes=[pltpu.SemaphoreType.DMA],
        name="slots",
    )(pattern.T, incoming)
    count = lax.dynamic_index_in_dim(counts, lax.axis_index("ctx"), 0, keepdims=False)
    group = q.shape[1] // d
    q = q.reshape(block, group, d)
    scale = 1.0 / math.sqrt(d)
    carried = (
        jnp.full((group, block), -jnp.inf, jnp.float32),
        jnp.zeros((group, block), jnp.float32),
        jnp.zeros((group, block, d), jnp.float32),
    )
    causal = jnp.arange(block)[:, None] >= jnp.arange(block)[None, :]
    carried = absorb(carried, q, kv, causal, scale)
    batch = math.gcd(width, 4)

    def step(at, carried):
        some = lax.dynamic_slice_in_dim(slots, at * batch, batch, 0).reshape(batch * block, 2 * d)
        usable = at * batch + jnp.arange(batch * block) // block < count
        return absorb(carried, q, some, usable, scale)

    _, denom, weighted = lax.fori_loop(0, width // batch, step, carried)
    result = (weighted / denom[..., None]).transpose(1, 0, 2).reshape(block, group * d)
    return lax.all_to_all(result.astype(jnp.bfloat16), "head", split_axis=0, concat_axis=1, tiled=True)


def solution(mesh):
    n_ctx, n_head = mesh.shape["ctx"], mesh.shape["head"]
    form = direct if (n_ctx, n_head) == (4, 4) else general
    return jax.shard_map(
        functools.partial(form, n_ctx, n_head),
        mesh=mesh,
        in_specs=(
            P(("grp", "ctx", "head"), None),
            P(("grp", "ctx", "head"), None),
            P("head", ("grp", "ctx"), None),
            P("grp", None),
            P("grp"),
        ),
        out_specs=P(("grp", "ctx", "head"), None),
        check_vma=False,
    )
```
